32 devices in a mesh: shot: 8 (over z, x), freq: 4 (over y, core).
Axes of the slice: x: 2, y: 2, z: 4, core: 2. Of those that a mesh axis runs over, the one named last changes fastest.
Arguments:
- data: bfloat16 [4, 2, 1024, 8192], P('freq', None, 'shot'), may hold values from -6 to 6
- primaries: bfloat16 [4, 2, 1024, 640], P('freq', None, 'shot'), may hold values from -0.15625 to 0.15625
- wavelet: float32 [4, 2], P('freq'), may hold values from 2 to 8
- cover_ids: int32 [1024, 8], P('shot'), may hold values from 0 to 15, all different within a row
- cover_counts: int32 [1024], P('shot'), may hold values from 1 to 8
Outputs:
- misfit: bfloat16 [4, 2, 1024, 8192], P('freq', None, 'shot')
- grad_primaries: float32 [4, 2, 1024, 640], P('freq', None, 'shot')
- wavelet_grad: float32 [128], replicated
The draws below stay inside these ranges and needn't reach their ends.
Inputs may be any that keep to these rules, and one draw needn't show every extreme that they name: `cover_ids`: the entries of a shot's list are different coverage blocks.
All inputs are finite; a program needn't handle non-finite values.
Results may differ from the reference program's by a relative error of at most 0.0013.
Values may be sent and summed in bfloat16 or wider, within the bound.
No kernel may reach another device: no remote copies, remote signals or barrier semaphores. Data moves between devices by JAX's collectives and lax.ppermute only.
A program may use at most 128 MiB of HBM per device.

```python
import math
import jax
import jax.numpy as jnp
from jax import lax

NR = 8192
SD = 128
REACH = 2
RB = 512
CMAX = 8
NT = 128
NS = 1024
NF = 4
BAND = 640
STRIDE = 8
NRB = 16


def with_ends(result, stream_key, smallest, largest):
    shape = result.shape
    spot = [jax.random.randint(jax.random.fold_in(stream_key, axis), (), 0, shape[axis]) for axis in range(len(shape))]
    result = result.at[tuple(spot)].set(smallest)
    longest = shape.index(max(shape))
    spot[longest] = (spot[longest] + 1) % shape[longest]
    return result.at[tuple(spot)].set(largest)


def block_scale(stream_key, shape, shards, low, high):
    factor_of, own = 1.0, jax.random.fold_in(stream_key, 6)
    for axis_at, shards_of in shards:
        draws = jnp.exp(jax.random.uniform(jax.random.fold_in(own, axis_at), (shards_of,), jnp.float32, low / len(shards), high / len(shards)))
        factor_of = factor_of * jnp.repeat(draws, shape[axis_at] // shards_of).reshape([-1 if axis == axis_at else 1 for axis in range(len(shape))])
    return factor_of


def picks_of(key, rows, count, top, lift):
    sequence = jax.random.permutation(jax.random.fold_in(key, 1), count)
    boost = sequence
    for power in range(3):
        boost = boost * boost // count
    boost = boost * lift // count
    chance = jax.random.randint(jax.random.fold_in(key, 2), (rows, count), 0, 4096) + boost
    sure = jax.random.permutation(jax.random.fold_in(key, 3), rows)[jnp.arange(count) % rows]
    chance = jnp.where(jnp.arange(rows)[:, None] == sure[None, :], 1 << 14, chance)
    score = chance * count + jnp.arange(count)
    return lax.top_k(score.astype(jnp.int32), top)[1].astype(jnp.int32)


def centred(own_key, shape, width, bound, cuts=(), held_as=jnp.bfloat16):
    array = jax.random.normal(own_key, shape, jnp.float32) * width
    if len(cuts) > 0:
        array = block_scale(own_key, shape, cuts, -0.22, 0.18) * array
    return jnp.clip(array, min=-bound, max=bound).astype(held_as)


def setup_inputs(seed: int = 0) -> dict:
    arg_keys = jax.random.split(jax.random.key(seed), 6)
    data = centred(arg_keys[0], (NF, 2, NS, NR), 1.0, 6.0, ((0, 4), (2, 8)))
    primaries = centred(arg_keys[1], (NF, 2, NS, BAND), (2 * BAND) ** -0.5, 0.15625, ((0, 4), (2, 8)))
    wavelet = jnp.clip(2.0 + 6.0 * jax.random.uniform(arg_keys[2], (NF, 2), jnp.float32) ** block_scale(arg_keys[2], (NF, 2), ((0, 4),), -0.2, 0.2), 2.0, 8.0)
    cover_ids = picks_of(arg_keys[3], NS, NRB, CMAX, 4096)
    cover_counts = with_ends(jax.random.randint(arg_keys[4], (NS,), 1, CMAX + 1), jax.random.fold_in(arg_keys[4], 1), 1, CMAX).astype(jnp.int32)
    return dict(data=data, primaries=primaries, wavelet=wavelet, cover_ids=cover_ids, cover_counts=cover_counts)


def reference(data, primaries, wavelet, cover_ids, cover_counts):
    block_count = NS // SD
    block_ids = jnp.arange(NRB, dtype=jnp.int32)
    listed = jnp.arange(CMAX, dtype=jnp.int32)[None, :] < cover_counts[:, None]
    covered = jnp.any((cover_ids[:, :, None] == block_ids[None, None, :]) & listed[:, :, None], axis=1).astype(jnp.float32)
    columns = jnp.arange(NR, dtype=jnp.int32)
    highest = lax.Precision.HIGHEST
    misfits = []
    gradients = []
    correlations = []
    for freq_index in range(NF):
        rows_padded = jnp.pad(data[freq_index], ((0, 0), (REACH * SD, REACH * SD), (0, 0)))
        wave_re = wavelet[freq_index, 0]
        wave_im = wavelet[freq_index, 1]
        response_all = primaries[freq_index]
        record_all = data[freq_index]

        def one_block(block):
            start = (block * SD).astype(jnp.int32)
            nearby = lax.dynamic_slice(rows_padded, (jnp.int32(0), start, jnp.int32(0)), (2, BAND, NR)).astype(jnp.float32)
            shot_ids = start - REACH * SD + jnp.arange(BAND, dtype=jnp.int32)
            direct_hit = columns[None, :] == shot_ids[:, None] * STRIDE
            operand = jnp.stack([jnp.where(direct_hit, wave_re, 0.0) - nearby[0], jnp.where(direct_hit, wave_im, 0.0) - nearby[1]])
            operand = lax.optimization_barrier(operand.astype(jnp.bfloat16)).astype(jnp.float32)
            response = lax.dynamic_slice(response_all, (jnp.int32(0), start, jnp.int32(0)), (2, SD, BAND)).astype(jnp.float32)
            pred_re = jnp.dot(response[0], operand[0], precision=highest) - jnp.dot(response[1], operand[1], precision=highest)
            pred_im = jnp.dot(response[0], operand[1], precision=highest) + jnp.dot(response[1], operand[0], precision=highest)
            record = lax.dynamic_slice(record_all, (jnp.int32(0), start, jnp.int32(0)), (2, SD, NR)).astype(jnp.float32)
            mask = jnp.repeat(lax.dynamic_slice(covered, (start, jnp.int32(0)), (SD, NRB)), RB, axis=1)
            misfit = (mask[None] * (record - jnp.stack([pred_re, pred_im]))).astype(jnp.bfloat16)
            resid = lax.optimization_barrier(misfit).astype(jnp.float32)
            grad_re = -(jnp.dot(resid[0], operand[0].T, precision=highest) + jnp.dot(resid[1], operand[1].T, precision=highest))
            grad_im = -(jnp.dot(resid[1], operand[0].T, precision=highest) - jnp.dot(resid[0], operand[1].T, precision=highest))
            sources = jnp.pad(resid[:, :, ::STRIDE], ((0, 0), (0, 0), (REACH * SD, REACH * SD)))
            sources = lax.dynamic_slice(sources, (jnp.int32(0), jnp.int32(0), start), (2, SD, BAND))
            corr_re = -jnp.sum(response[0] * sources[0] + response[1] * sources[1])
            corr_im = -jnp.sum(response[0] * sources[1] - response[1] * sources[0])
            return (misfit, jnp.stack([grad_re, grad_im]), jnp.stack([corr_re, corr_im]))
        errs, grads, corr = lax.map(one_block, jnp.arange(block_count, dtype=jnp.int32))
        misfits.append(jnp.transpose(errs, (1, 0, 2, 3)).reshape(2, NS, NR))
        gradients.append(jnp.transpose(grads, (1, 0, 2, 3)).reshape(2, NS, BAND))
        correlations.append(lax.optimization_barrier(jnp.sum(corr, axis=0)))
    times = jnp.arange(NT, dtype=jnp.int32).astype(jnp.float32)
    series = jnp.zeros((NT,), jnp.float32)
    for freq_index in range(NF):
        phase = 2.0 * math.pi * (freq_index + 1) * times / NT
        series = series + correlations[freq_index][0] * jnp.cos(phase) - correlations[freq_index][1] * jnp.sin(phase)
    wavelet_grad = series / math.sqrt(NS * BAND)
    return (jnp.stack(misfits), jnp.stack(gradients), wavelet_grad)
```

```python
import functools
import math

import jax
import jax.numpy as jnp
from jax import lax
from jax.experimental import pallas as pl
from jax.experimental.pallas import tpu as pltpu
from jax.sharding import PartitionSpec as P

RB = 512
NT = 128
VMEM = 48 * 1024 * 1024
PARTS = (2, 4, 4, 4, 2)
LOW, LOW_X, OWN, MATE, HIGH, HIGH_X = range(6)


def split_kernel(half, cuts, info, whole, *refs):
    outs, sems = refs[:-1], refs[-1]
    side = info[0]
    copies = []
    for n, (off, size) in enumerate(cuts):
        for which in range(2):
            start = (side if which == 0 else 1 - side) * half + off
            copies.append(
                pltpu.make_async_copy(
                    whole.at[:, :, pl.ds(pl.multiple_of(start, 128), size)],
                    outs[2 * n + which],
                    sems.at[2 * n + which],
                )
            )
    for copy in copies:
        copy.start()
    for copy in copies:
        copy.wait()


def split(info, whole, half, cuts):
    rows = whole.shape[1]
    shapes = [
        jax.ShapeDtypeStruct((2, rows, size), whole.dtype) for _, size in cuts for _ in range(2)
    ]
    outs = pl.pallas_call(
        functools.partial(split_kernel, half, cuts),
        out_shape=shapes,
        in_specs=[pl.BlockSpec(memory_space=pltpu.SMEM), pl.BlockSpec(memory_space=pl.ANY)],
        out_specs=[pl.BlockSpec(memory_space=pl.ANY)] * len(shapes),
        scratch_shapes=[pltpu.SemaphoreType.DMA((len(shapes),))],
        cost_estimate=pl.CostEstimate(
            flops=0, bytes_accessed=sum(8 * rows * size * 2 for _, size in cuts), transcendentals=0
        ),
        name="split_columns",
    )(info, whole)
    return [(outs[2 * n], outs[2 * n + 1]) for n in range(len(cuts))]


def place_kernel(half, off, size, info, whole_in, part, whole, sem):
    del whole_in
    start = (1 - info[0]) * half + off
    copy = pltpu.make_async_copy(
        part, whole.at[:, :, pl.ds(pl.multiple_of(start, 128), size)], sem
    )
    copy.start()
    copy.wait()


def place(info, whole, part, half, off):
    size = part.shape[2]
    return pl.pallas_call(
        functools.partial(place_kernel, half, off, size),
        out_shape=jax.ShapeDtypeStruct(whole.shape, whole.dtype),
        in_specs=[pl.BlockSpec(memory_space=pltpu.SMEM)] + [pl.BlockSpec(memory_space=pl.ANY)] * 2,
        out_specs=pl.BlockSpec(memory_space=pl.ANY),
        scratch_shapes=[pltpu.SemaphoreType.DMA],
        input_output_aliases={1: 0},
        cost_estimate=pl.CostEstimate(
            flops=0, bytes_accessed=2 * part.size * 2, transcendentals=0
        ),
        name="place_columns",
    )(info, whole, part)


def chunk_kernel(conf, *refs):
    rows, tile, steps, stride, off, half, layout, first = conf
    refs = list(refs)
    info, wave, resp, ids = (refs.pop(0) for _ in range(4))
    count = max(ref for ref, _ in layout) + 1
    tiles = [refs.pop(0) for _ in range(count)]
    if not first:
        _, grad_in, corr_in = (refs.pop(0) for _ in range(3))
    out_own, out_mate, grad_out, corr_out, ys, sums = refs
    step = pl.program_id(0)
    side, pos = info[0], info[1]
    mate = pos + 1 - 2 * side
    width2 = 2 * rows
    col0 = side * half + off + step * tile
    blocks = (pos - 2, mate - 2, pos, mate, pos + 2, mate + 2)

    @pl.when(step == 0)
    def _():
        sums[...] = jnp.zeros_like(sums)
        corr_out[...] = jnp.zeros_like(corr_out) if first else corr_in[...]

    def record(slot):
        ref, part = layout[slot]
        value = tiles[ref][...] if part is None else tiles[ref][part]
        return value.reshape(width2, tile)

    def hits(slot):
        shots = blocks[slot] * rows + lax.broadcasted_iota(jnp.int32, (rows, tile), 0)
        cols = col0 + lax.broadcasted_iota(jnp.int32, (rows, tile), 1)
        return shots * stride == cols

    def meets(slot):
        low = blocks[slot] * rows * stride
        return (low < col0 + tile) & (low + rows * stride > col0)

    for slot in range(6):
        ys[pl.ds(slot * width2, width2), :] = record(slot)

        @pl.when(meets(slot))
        def _(slot=slot):
            hit = hits(slot)
            for c in range(2):
                at = pl.ds(slot * width2 + c * rows, rows)
                direct = jnp.where(hit, wave[c], 0.0)
                ys[at, :] = (ys[at, :].astype(jnp.float32) - direct).astype(jnp.bfloat16)

    y = ys[...]
    fit = jnp.dot(resp[...], y, preferred_element_type=jnp.float32)
    lists = ids[...]
    entry = lax.broadcasted_iota(jnp.int32, lists.shape, 1)
    count_col = lists[:, -1:]
    recorded = (lists == col0 // RB) & (entry < count_col) & (entry < lists.shape[1] - 1)
    covered = jnp.max(jnp.where(recorded, 1.0, 0.0), axis=1, keepdims=True)
    out = []
    for which, slot in ((0, OWN), (1, MATE)):
        mask = covered[which * rows : (which + 1) * rows]
        mask = jnp.concatenate([mask, mask], axis=0)
        value = record(slot).astype(jnp.float32) + fit[which * width2 : (which + 1) * width2]
        out.append((mask * value).astype(jnp.bfloat16))
    out_own[...] = out[0].reshape(out_own.shape)
    out_mate[...] = out[1].reshape(out_mate.shape)
    misfit = jnp.concatenate(out, axis=0)
    across = (((1,), (1,)), ((), ()))
    sums[...] += lax.dot_general(misfit, y, across, preferred_element_type=jnp.float32)

    for slot in range(6):

        @pl.when(meets(slot))
        def _(slot=slot):
            one = jnp.where(hits(slot), 1.0, 0.0).astype(jnp.bfloat16)
            at_shots = lax.dot_general(misfit, one, across, preferred_element_type=jnp.float32)
            for c in range(2):
                x = resp[:, pl.ds(slot * width2 + c * rows, rows)].astype(jnp.float32)
                terms = (x * at_shots).reshape(-1, 8, rows)
                corr_out[c] -= jnp.sum(terms, axis=0)

    @pl.when(step == steps - 1)
    def _():
        even = side == 0
        for which in range(2):
            re = pl.ds(which * width2, rows)
            im = pl.ds(which * width2 + rows, rows)

            def part(slot):
                a = pl.ds(slot * width2, rows)
                b = pl.ds(slot * width2 + rows, rows)
                return (sums[re, a] + sums[im, b], sums[im, a] - sums[re, b])

            if which == 0:
                order = (LOW, (LOW_X, MATE), OWN, (MATE, HIGH_X), HIGH)
            else:
                order = (LOW_X, (OWN, LOW), MATE, (HIGH, OWN), HIGH_X)
            for k, slot in enumerate(order):
                at = pl.ds(k * rows, rows)
                if isinstance(slot, tuple):
                    value = [
                        jnp.where(even, p, q) for p, q in zip(part(slot[0]), part(slot[1]))
                    ]
                else:
                    value = part(slot)
                for c in range(2):
                    if first:
                        grad_out[which, c, :, at] = value[c]
                    else:
                        grad_out[which, c, :, at] = grad_in[which, c, :, at] + value[c]


def chunk(info, wave, resp, ids, arrays, layout, carry, off, size, half, width, stride, rows, band):
    tile = min(size, RB)
    steps = size // tile
    first = carry is None
    conf = (rows, tile, steps, stride, off, half, layout, first)
    whole_block = pl.BlockSpec(
        (2, rows, tile), lambda i, info: (0, 0, (info[0] * half + off) // tile + i)
    )
    grad_shape = (2, 2, rows, band)
    corr_shape = (2, 8, rows)

    def full(shape):
        return pl.BlockSpec(shape, lambda i, info: (0,) * len(shape))

    in_specs = [pl.BlockSpec(memory_space=pltpu.SMEM), full(resp.shape), full(ids.shape)]
    for a in arrays:
        if a.ndim == 3:
            in_specs.append(pl.BlockSpec((2, rows, tile), lambda i, info: (0, 0, i)))
        else:
            in_specs.append(pl.BlockSpec((2, 2, rows, tile), lambda i, info: (0, 0, 0, i)))
    args = [info, wave, resp, ids, *arrays]
    aliases = {}
    if not first:
        aliases = {len(args): 0, len(args) + 1: 2, len(args) + 2: 3}
        args += list(carry)
        in_specs += [pl.BlockSpec(memory_space=pl.ANY), full(grad_shape), full(corr_shape)]
    macs = 2 * resp.shape[0] * resp.shape[1] * size
    return pl.pallas_call(
        functools.partial(chunk_kernel, conf),
        out_shape=[
            jax.ShapeDtypeStruct((2, rows, width), jnp.bfloat16),
            jax.ShapeDtypeStruct((2, rows, size), jnp.bfloat16),
            jax.ShapeDtypeStruct(grad_shape, jnp.float32),
            jax.ShapeDtypeStruct(corr_shape, jnp.float32),
        ],
        grid_spec=pltpu.PrefetchScalarGridSpec(
            num_scalar_prefetch=1,
            grid=(steps,),
            in_specs=in_specs,
            out_specs=[
                whole_block,
                pl.BlockSpec((2, rows, tile), lambda i, info: (0, 0, i)),
                full(grad_shape),
                full(corr_shape),
            ],
            scratch_shapes=[
                pltpu.VMEM((12 * rows, tile), jnp.bfloat16),
                pltpu.VMEM((4 * rows, 12 * rows), jnp.float32),
            ],
        ),
        input_output_aliases=aliases,
        compiler_params=pltpu.CompilerParams(vmem_limit_bytes=VMEM),
        cost_estimate=pl.CostEstimate(
            flops=2 * macs, bytes_accessed=16 * rows * size * 2 + 5 * 10**6, transcendentals=0
        ),
        name="residual_chunk",
    )(*args)


def responses(own, mate, side, rows):
    even = side == 0

    def piece(a, k):
        return a[:, :, k * rows : (k + 1) * rows]

    none = jnp.zeros_like(piece(own, 0))
    o = [piece(own, k) for k in range(5)]
    m = [piece(mate, k) for k in range(5)]
    table = [
        [o[0], jnp.where(even, o[1], none), o[2], jnp.where(even, o[3], o[1]), o[4],
         jnp.where(even, none, o[3])],
        [jnp.where(even, none, m[1]), m[0], jnp.where(even, m[1], m[3]), m[2],
         jnp.where(even, m[3], none), m[4]],
    ]
    lines = []
    for line in table:
        lines.append(jnp.concatenate([v for p in line for v in (p[0], -p[1])], axis=1))
        lines.append(jnp.concatenate([v for p in line for v in (p[1], p[0])], axis=1))
    return jnp.concatenate(lines, axis=0)


def on_device(data, primaries, wavelet, cover_ids, cover_counts):
    record = data[0]
    _, rows, width = record.shape
    band = primaries.shape[3]
    devices = lax.axis_size("shot")
    shot_count = devices * rows
    stride = width // shot_count
    half = width // 2
    position = lax.axis_index("shot").astype(jnp.int32)
    freq_index = lax.axis_index("freq")
    side = position % 2
    info = jnp.stack([side, position])
    unit = half // sum(PARTS)
    cuts, off = [], 0
    for part in PARTS:
        cuts.append((off, part * unit))
        off += part * unit

    swap = [(i, i ^ 1) for i in range(devices)]
    up = [(i, i + 2) for i in range(devices - 2)]
    down = [(i + 2, i) for i in range(devices - 2)]

    def send(a, route):
        return lax.ppermute(a, "shot", route)

    pieces = split(info, record, half, cuts[:1]) + split(info, record, half, cuts[1:])
    response = primaries[0]
    lists = jnp.concatenate([cover_ids, cover_counts[:, None]], axis=1)
    resp = responses(response, send(response, swap), side, rows)
    ids = jnp.concatenate([lists, send(lists, swap)], axis=0)
    wave = wavelet[0]

    carry = None
    for n, (off, size) in enumerate(cuts):
        mine, other = pieces[n]
        theirs = send(other, swap)
        if n == 0:
            arrays = [
                mine, theirs, send(mine, up), send(theirs, up), send(mine, down), send(theirs, down)
            ]
            layout = ((2, None), (3, None), (0, None), (1, None), (4, None), (5, None))
        else:
            both = jnp.stack([mine, theirs])
            arrays = [both, send(both, up), send(both, down)]
            layout = ((1, 0), (1, 1), (0, 0), (0, 1), (2, 0), (2, 1))
        whole, back, grad, corr = chunk(
            info, wave, resp, ids, arrays, layout, carry,
            off, size, half, width, stride, rows, band,
        )
        whole = place(info, whole, send(back, swap), half, off)
        carry = (whole, grad, corr)

    gradient = grad[0] + send(grad[1], swap)
    total_re, total_im = jnp.sum(corr[0]), jnp.sum(corr[1])
    times = jnp.arange(NT, dtype=jnp.int32).astype(jnp.float32)
    phase = 2.0 * math.pi * (freq_index + 1).astype(jnp.float32) * times / NT
    scale = 1.0 / math.sqrt(shot_count * band)
    series = total_re * jnp.cos(phase) - total_im * jnp.sin(phase)
    wavelet_grad = lax.psum(series, ("shot", "freq")) * scale
    return (whole[None], gradient[None], wavelet_grad)


def solution(mesh):
    in_specs = (
        P("freq", None, "shot", None),
        P("freq", None, "shot", None),
        P("freq", None),
        P("shot", None),
        P("shot"),
    )
    out_specs = (P("freq", None, "shot", None), P("freq", None, "shot", None), P())
    return jax.shard_map(
        on_device, mesh=mesh, in_specs=in_specs, out_specs=out_specs, check_vma=False
    )
```

```python
import functools
import math

import jax
import jax.numpy as jnp
from jax import lax
from jax.experimental import pallas as pl
from jax.experimental.pallas import tpu as pltpu
from jax.sharding import PartitionSpec as P

RB = 512
NT = 128
VMEM = 20 * 1024 * 1024
PARTS = (2, 4, 4, 4, 2)
LOW, LOW_X, OWN, MATE, HIGH, HIGH_X = range(6)
IN_SMEM = pl.BlockSpec(memory_space=pltpu.SMEM)
IN_VMEM = pl.BlockSpec(memory_space=pltpu.VMEM)
ANYWHERE = pl.BlockSpec(memory_space=pl.ANY)


def split_kernel(half, off, size, info, whole, mine, other, sems):
    side = info[0]
    copies = []
    for which, out in ((0, mine), (1, other)):
        start = (side if which == 0 else 1 - side) * half + off
        source = whole.at[:, :, pl.ds(pl.multiple_of(start, 128), size)]
        copies.append(pltpu.make_async_copy(source, out, sems.at[which]))
    for copy in copies:
        copy.start()
    for copy in copies:
        copy.wait()


def split(info, whole, half, off, size):
    rows = whole.shape[1]
    piece = jax.ShapeDtypeStruct((2, rows, size), whole.dtype)
    return pl.pallas_call(
        functools.partial(split_kernel, half, off, size),
        out_shape=[piece, piece],
        in_specs=[IN_SMEM, ANYWHERE],
        out_specs=[IN_VMEM, IN_VMEM],
        scratch_shapes=[pltpu.SemaphoreType.DMA((2,))],
        compiler_params=pltpu.CompilerParams(vmem_limit_bytes=VMEM),
        cost_estimate=pl.CostEstimate(
            flops=0, bytes_accessed=8 * rows * size * 2, transcendentals=0
        ),
        name="split_columns",
    )(info, whole)


def place_kernel(half, off, size, info, whole_in, part, whole, sem):
    del whole_in
    start = (1 - info[0]) * half + off
    copy = pltpu.make_async_copy(
        part, whole.at[:, :, pl.ds(pl.multiple_of(start, 128), size)], sem
    )
    copy.start()
    copy.wait()


def place(info, whole, part, half, off):
    size = part.shape[2]
    return pl.pallas_call(
        functools.partial(place_kernel, half, off, size),
        out_shape=jax.ShapeDtypeStruct(whole.shape, whole.dtype),
        in_specs=[IN_SMEM, ANYWHERE, IN_VMEM],
        out_specs=ANYWHERE,
        scratch_shapes=[pltpu.SemaphoreType.DMA],
        input_output_aliases={1: 0},
        compiler_params=pltpu.CompilerParams(vmem_limit_bytes=VMEM),
        cost_estimate=pl.CostEstimate(
            flops=0, bytes_accessed=2 * part.size * 2, transcendentals=0
        ),
        name="place_columns",
    )(info, whole, part)


def chunk_kernel(conf, *refs):
    rows, size, stride, off, half, layout, first = conf
    refs = list(refs)
    info, wave, resp, ids = (refs.pop(0) for _ in range(4))
    count = max(ref for ref, _ in layout) + 1
    given = [refs.pop(0) for _ in range(count)]
    if not first:
        _, grad_in, corr_in = (refs.pop(0) for _ in range(3))
    whole, out_mate, grad_out, corr_out, ys, ms, out_own, sem = refs
    side, pos = info[0], info[1]
    mate = pos + 1 - 2 * side
    col0 = side * half + off
    blocks = (pos - 2, mate - 2, pos, mate, pos + 2, mate + 2)
    tile = min(size, RB)

    def record(slot, c, cols):
        ref, part = layout[slot]
        return given[ref][c, :, cols] if part is None else given[ref][part, c, :, cols]

    def hits(slot):
        shots = blocks[slot] * rows + lax.broadcasted_iota(jnp.int32, (rows, size), 0)
        cols = col0 + lax.broadcasted_iota(jnp.int32, (rows, size), 1)
        return shots * stride == cols

    def meets(slot):
        low = blocks[slot] * rows * stride
        return (low < col0 + size) & (low + rows * stride > col0)

    for slot in range(6):
        at = slice(slot * rows, (slot + 1) * rows)
        for c in range(2):
            ys[at, c * size : (c + 1) * size] = record(slot, c, slice(None))

        @pl.when(meets(slot))
        def _(slot=slot, at=at):
            hit = hits(slot)
            for c in range(2):
                cols = slice(c * size, (c + 1) * size)
                direct = jnp.where(hit, wave[c], 0.0)
                ys[at, cols] = (ys[at, cols].astype(jnp.float32) - direct).astype(jnp.bfloat16)

    lists = ids[...]
    entry = lax.broadcasted_iota(jnp.int32, lists.shape, 1)
    listed = (entry < lists[:, -1:]) & (entry < lists.shape[1] - 1)
    for t in range(size // tile):
        cols = slice(t * tile, (t + 1) * tile)
        cols_im = slice(size + t * tile, size + (t + 1) * tile)
        y = jnp.concatenate([ys[:, cols], ys[:, cols_im]], axis=0)
        fit = jnp.dot(resp[...], y, preferred_element_type=jnp.float32)
        recorded = listed & (lists == (col0 + t * tile) // RB)
        covered = jnp.max(jnp.where(recorded, 1.0, 0.0), axis=1, keepdims=True)
        for which, slot in ((0, OWN), (1, MATE)):
            mask = covered[which * rows : (which + 1) * rows]
            pair = []
            for c in range(2):
                at = which * 2 + c
                value = record(slot, c, cols).astype(jnp.float32) + fit[at * rows : (at + 1) * rows]
                pair.append((mask * value).astype(jnp.bfloat16))
                (out_own if which == 0 else out_mate)[c, :, cols] = pair[c]
            at = slice(which * 2 * rows, (which * 2 + 1) * rows)
            ms[at, cols] = pair[0]
            ms[at, cols_im] = pair[1]
            at = slice((which * 2 + 1) * rows, (which * 2 + 2) * rows)
            ms[at, cols] = pair[1]
            ms[at, cols_im] = -pair[0]
    copy = pltpu.make_async_copy(
        out_own, whole.at[:, :, pl.ds(pl.multiple_of(col0, 128), size)], sem
    )
    copy.start()
    across = (((1,), (1,)), ((), ()))
    total = lax.dot_general(ms[...], ys[...], across, preferred_element_type=jnp.float32)
    grad_out[...] = total if first else grad_in[...] + total
    corr_out[...] = jnp.zeros_like(corr_out) if first else corr_in[...]

    for slot in range(6):

        @pl.when(meets(slot))
        def _(slot=slot):
            one = jnp.where(hits(slot), 1.0, 0.0).astype(jnp.bfloat16)
            at_shots = lax.dot_general(
                ms[:, :size], one, across, preferred_element_type=jnp.float32
            )
            for c in range(2):
                at = c * 6 * rows + slot * rows
                x = resp[:, at : at + rows].astype(jnp.float32)
                terms = (x * at_shots).reshape(-1, 8, rows)
                corr_out[c] -= jnp.sum(terms, axis=0)

    copy.wait()


def chunk(info, wave, resp, ids, arrays, layout, carry, off, size, half, width, stride, rows, band):
    first = carry is None
    conf = (rows, size, stride, off, half, layout, first)
    args = [info, wave, resp, ids, *arrays]
    in_specs = [IN_SMEM, IN_SMEM] + [IN_VMEM] * (2 + len(arrays))
    aliases = {}
    if not first:
        aliases = {len(args): 0, len(args) + 1: 2, len(args) + 2: 3}
        args += list(carry)
        in_specs += [ANYWHERE, IN_VMEM, IN_VMEM]
    macs = 2 * resp.shape[0] * resp.shape[1] * size
    return pl.pallas_call(
        functools.partial(chunk_kernel, conf),
        out_shape=[
            jax.ShapeDtypeStruct((2, rows, width), jnp.bfloat16),
            jax.ShapeDtypeStruct((2, rows, size), jnp.bfloat16),
            jax.ShapeDtypeStruct((4 * rows, 6 * rows), jnp.float32),
            jax.ShapeDtypeStruct((2, 8, rows), jnp.float32),
        ],
        in_specs=in_specs,
        out_specs=[ANYWHERE, IN_VMEM, IN_VMEM, IN_VMEM],
        scratch_shapes=[
            pltpu.VMEM((6 * rows, 2 * size), jnp.bfloat16),
            pltpu.VMEM((4 * rows, 2 * size), jnp.bfloat16),
            pltpu.VMEM((2, rows, size), jnp.bfloat16),
            pltpu.SemaphoreType.DMA,
        ],
        input_output_aliases=aliases,
        compiler_params=pltpu.CompilerParams(vmem_limit_bytes=VMEM),
        cost_estimate=pl.CostEstimate(
            flops=2 * macs, bytes_accessed=16 * rows * size * 2, transcendentals=0
        ),
        name="residual_chunk",
    )(*args)


def in_band_order(grad, side, rows):
    even = side == 0
    slots = [grad[:, s * rows : (s + 1) * rows].reshape(2, 2, rows, rows) for s in range(6)]

    def pick(which, a, b):
        return jnp.where(even, slots[a][which], slots[b][which])

    own = [slots[LOW][0], pick(0, LOW_X, MATE), slots[OWN][0], pick(0, MATE, HIGH_X), slots[HIGH][0]]
    mate = [
        slots[LOW_X][1], pick(1, OWN, LOW), slots[MATE][1], pick(1, HIGH, OWN), slots[HIGH_X][1]
    ]
    return jnp.concatenate(own, axis=2), jnp.concatenate(mate, axis=2)


def total_over(value, axis):
    size = lax.axis_size(axis)
    if size & (size - 1):
        return lax.psum(value, axis)
    step = 1
    while step < size:
        value = value + lax.ppermute(value, axis, [(i, i ^ step) for i in range(size)])
        step *= 2
    return value


def responses(own, mate, side, rows):
    even = side == 0

    def piece(a, k):
        return a[:, :, k * rows : (k + 1) * rows]

    none = jnp.zeros_like(piece(own, 0))
    o = [piece(own, k) for k in range(5)]
    m = [piece(mate, k) for k in range(5)]
    table = [
        [o[0], jnp.where(even, o[1], none), o[2], jnp.where(even, o[3], o[1]), o[4],
         jnp.where(even, none, o[3])],
        [jnp.where(even, none, m[1]), m[0], jnp.where(even, m[1], m[3]), m[2],
         jnp.where(even, m[3], none), m[4]],
    ]
    lines = []
    for line in table:
        lines.append(jnp.concatenate([p[0] for p in line] + [-p[1] for p in line], axis=1))
        lines.append(jnp.concatenate([p[1] for p in line] + [p[0] for p in line], axis=1))
    return jnp.concatenate(lines, axis=0)


def on_device(data, primaries, wavelet, cover_ids, cover_counts):
    record = data[0]
    _, rows, width = record.shape
    band = primaries.shape[3]
    devices = lax.axis_size("shot")
    shot_count = devices * rows
    stride = width // shot_count
    half = width // 2
    position = lax.axis_index("shot").astype(jnp.int32)
    freq_index = lax.axis_index("freq")
    side = position % 2
    info = jnp.stack([side, position])
    unit = half // sum(PARTS)
    cuts, off = [], 0
    for part in PARTS:
        cuts.append((off, part * unit))
        off += part * unit

    swap = [(i, i ^ 1) for i in range(devices)]
    up = [(i, i + 2) for i in range(devices - 2)]
    down = [(i + 2, i) for i in range(devices - 2)]

    def send(a, route):
        return lax.ppermute(a, "shot", route)

    pieces = [split(info, record, half, off, size) for off, size in cuts]
    response = primaries[0]
    lists = jnp.concatenate([cover_ids, cover_counts[:, None]], axis=1)
    resp = responses(response, send(response, swap), side, rows)
    ids = jnp.concatenate([lists, send(lists, swap)], axis=0)
    wave = wavelet[0]

    carry = None
    for n, (off, size) in enumerate(cuts):
        mine, other = pieces[n]
        theirs = send(other, swap)
        if n == 0:
            arrays = [
                mine, theirs, send(mine, up), send(theirs, up), send(mine, down), send(theirs, down)
            ]
            layout = ((2, None), (3, None), (0, None), (1, None), (4, None), (5, None))
        else:
            both = jnp.stack([mine, theirs])
            arrays = [both, send(both, up), send(both, down)]
            layout = ((1, 0), (1, 1), (0, 0), (0, 1), (2, 0), (2, 1))
        whole, back, grad, corr = chunk(
            info, wave, resp, ids, arrays, layout, carry,
            off, size, half, width, stride, rows, band,
        )
        whole = place(info, whole, send(back, swap), half, off)
        carry = (whole, grad, corr)

    grad_own, grad_mate = in_band_order(grad, side, rows)
    gradient = grad_own + send(grad_mate, swap)
    total_re, total_im = jnp.sum(corr[0]), jnp.sum(corr[1])
    times = jnp.arange(NT, dtype=jnp.int32).astype(jnp.float32)
    phase = 2.0 * math.pi * (freq_index + 1).astype(jnp.float32) * times / NT
    scale = 1.0 / math.sqrt(shot_count * band)
    series = total_re * jnp.cos(phase) - total_im * jnp.sin(phase)
    wavelet_grad = total_over(total_over(series, "freq"), "shot") * scale
    return (whole[None], gradient[None], wavelet_grad)


def solution(mesh):
    in_specs = (
        P("freq", None, "shot", None),
        P("freq", None, "shot", None),
        P("freq", None),
        P("shot", None),
        P("shot"),
    )
    out_specs = (P("freq", None, "shot", None), P("freq", None, "shot", None), P())
    return jax.shard_map(
        on_device, mesh=mesh, in_specs=in_specs, out_specs=out_specs, check_vma=False
    )
```

```python
import functools
import math

import jax
import jax.numpy as jnp
from jax import lax
from jax.experimental import pallas as pl
from jax.experimental.pallas import tpu as pltpu
from jax.sharding import PartitionSpec as P

RB = 512
NT = 128
VMEM = 14 * 1024 * 1024
PARTS = (4, 4, 4, 2, 2)
GROUPS = ((0,), (1,), (2,), (3, 4))
LOW, LOW_X, OWN, MATE, HIGH, HIGH_X = range(6)
IN_SMEM = pl.BlockSpec(memory_space=pltpu.SMEM)
IN_VMEM = pl.BlockSpec(memory_space=pltpu.VMEM)
IN_HBM = pl.BlockSpec(memory_space=pltpu.HBM)
PARAMS = pltpu.CompilerParams(vmem_limit_bytes=VMEM)
LIGHT = pl.CostEstimate(flops=0, bytes_accessed=0, transcendentals=0)


def columns(ref, start, size):
    return ref.at[:, :, pl.ds(pl.multiple_of(start, 128), size)]


def run(copies):
    for copy in copies:
        copy.start()
    for copy in copies:
        copy.wait()


def split_kernel(half, off, size, other, info, whole, out, sem):
    side = 1 - info[0] if other else info[0]
    run([pltpu.make_async_copy(columns(whole, side * half + off, size), out, sem)])


def split(info, whole, half, off, size, other):
    return pl.pallas_call(
        functools.partial(split_kernel, half, off, size, other),
        out_shape=jax.ShapeDtypeStruct((*whole.shape[:2], size), whole.dtype),
        in_specs=[IN_SMEM, IN_HBM],
        out_specs=IN_VMEM,
        scratch_shapes=[pltpu.SemaphoreType.DMA],
        compiler_params=PARAMS,
        cost_estimate=LIGHT,
        name="split_columns",
    )(info, whole)


def join_kernel(half, cuts, info, whole, theirs, *refs):
    outs, sems = refs[:-1], refs[-1]
    base = cuts[0][0]
    copies = []
    for n, (off, size) in enumerate(cuts):
        mine = columns(whole, info[0] * half + off, size)
        copies.append(pltpu.make_async_copy(mine, outs[n].at[0], sems.at[2 * n]))
        got = theirs.at[:, :, pl.ds(off - base, size)]
        copies.append(pltpu.make_async_copy(got, outs[n].at[1], sems.at[2 * n + 1]))
    run(copies)


def join(info, whole, theirs, half, cuts):
    return pl.pallas_call(
        functools.partial(join_kernel, half, cuts),
        out_shape=[
            jax.ShapeDtypeStruct((2, *theirs.shape[:2], size), theirs.dtype) for _, size in cuts
        ],
        in_specs=[IN_SMEM, IN_HBM, IN_VMEM],
        out_specs=[IN_VMEM] * len(cuts),
        scratch_shapes=[pltpu.SemaphoreType.DMA((2 * len(cuts),))],
        compiler_params=PARAMS,
        cost_estimate=LIGHT,
        name="join_blocks",
    )(info, whole, theirs)


def place_kernel(half, off, size, info, here, there, *refs):
    whole, sems = refs[-2:]
    side = info[0]
    run(
        [
            pltpu.make_async_copy(here, columns(whole, side * half + off, size), sems.at[0]),
            pltpu.make_async_copy(there, columns(whole, (1 - side) * half + off, size), sems.at[1]),
        ]
    )


def place(info, here, there, whole, half, off):
    _, rows, size = here.shape
    first = whole is None
    return pl.pallas_call(
        functools.partial(place_kernel, half, off, size),
        out_shape=jax.ShapeDtypeStruct((2, rows, 2 * half), here.dtype),
        in_specs=[IN_SMEM, IN_VMEM, IN_VMEM] + ([] if first else [IN_HBM]),
        out_specs=IN_HBM,
        scratch_shapes=[pltpu.SemaphoreType.DMA((2,))],
        input_output_aliases={} if first else {3: 0},
        compiler_params=PARAMS,
        cost_estimate=LIGHT,
        name="place_columns",
    )(info, here, there, *([] if first else [whole]))


def prepare_kernel(info, own, mate, resp, mask):
    rows = mask.shape[0] // 2
    none = None
    tables = (
        ((0, 1, 2, 3, 4, none), (none, 0, 1, 2, 3, 4)),
        ((0, none, 2, 1, 4, 3), (1, 0, 3, 2, none, 4)),
    )
    for which, params in ((0, own), (1, mate)):
        mask[which * rows : (which + 1) * rows, :] = params[2 * rows :, :rows].astype(jnp.float32).T
        line = slice(2 * which * rows, (2 * which + 1) * rows)
        line_im = slice((2 * which + 1) * rows, (2 * which + 2) * rows)
        for side in range(2):

            @pl.when(info[0] == side)
            def _(params=params, line=line, line_im=line_im, table=tables[side][which]):
                for slot, k in enumerate(table):
                    at = slice(slot * rows, (slot + 1) * rows)
                    at_im = slice((6 + slot) * rows, (7 + slot) * rows)
                    if k is None:
                        re = im = jnp.zeros((rows, rows), resp.dtype)
                    else:
                        re = params[:rows, k * rows : (k + 1) * rows]
                        im = params[rows : 2 * rows, k * rows : (k + 1) * rows]
                    resp[line, at] = re
                    resp[line, at_im] = -im
                    resp[line_im, at] = im
                    resp[line_im, at_im] = re


def prepare(info, own, mate, rows):
    blocks = own.shape[0] - 2 * rows
    return pl.pallas_call(
        prepare_kernel,
        out_shape=[
            jax.ShapeDtypeStruct((4 * rows, 12 * rows), own.dtype),
            jax.ShapeDtypeStruct((2 * rows, blocks), jnp.float32),
        ],
        in_specs=[IN_SMEM, IN_VMEM, IN_VMEM],
        out_specs=[IN_VMEM, IN_VMEM],
        compiler_params=PARAMS,
        cost_estimate=LIGHT,
        name="prepare_response",
    )(info, own, mate)


def chunk_kernel(conf, *refs):
    rows, size, stride, half, off, band, layout, first, last = conf
    refs = list(refs)
    info, wave, waves, resp, mask = (refs.pop(0) for _ in range(5))
    given = [refs.pop(0) for _ in range(max(ref for ref, _ in layout) + 1)]
    if not first:
        grad_in, corr_in = refs.pop(0), refs.pop(0)
    out_own, out_mate = refs.pop(0), refs.pop(0)
    if last:
        grad_own, grad_mate, corr_out = (refs.pop(0) for _ in range(3))
    else:
        grad_out, corr_out = refs.pop(0), refs.pop(0)
    ys, ms, sums, corrs = refs
    side, pos = info[0], info[1]
    mate = pos + 1 - 2 * side
    blocks = (pos - 2, mate - 2, pos, mate, pos + 2, mate + 2)
    col0 = side * half + off
    tile = RB if (off | size) % RB == 0 else RB // 2

    def record(slot, c, cols=slice(None)):
        ref, part = layout[slot]
        return given[ref][c, :, cols] if part is None else given[ref][part, c, :, cols]

    def hits(slot, start):
        shots = blocks[slot] * rows + lax.broadcasted_iota(jnp.int32, (rows, tile), 0)
        cols = start + lax.broadcasted_iota(jnp.int32, (rows, tile), 1)
        return shots * stride == cols

    def meets(slot, start):
        low = blocks[slot] * rows * stride
        return (low < start + tile) & (low + rows * stride > start)

    for slot in range(6):
        at = slice(slot * rows, (slot + 1) * rows)
        for c in range(2):
            ys[at, c * size : (c + 1) * size] = record(slot, c)

    @pl.loop(0, size // tile)
    def _(t):
        for slot in range(6):

            @pl.when(meets(slot, col0 + t * tile))
            def _(slot=slot):
                hit = hits(slot, col0 + t * tile)
                at = slice(slot * rows, (slot + 1) * rows)
                for c in range(2):
                    cols = pl.ds(pl.multiple_of(c * size + t * tile, tile), tile)
                    direct = jnp.where(hit, wave[c], 0.0)
                    ys[at, cols] = (ys[at, cols].astype(jnp.float32) - direct).astype(jnp.bfloat16)

    across = (((1,), (1,)), ((), ()))
    corrs[...] = jnp.zeros_like(corrs) if first else corr_in[...]
    listed = mask[...]
    receiver_block = lax.broadcasted_iota(jnp.int32, listed.shape, 1)
    for t in range(size // tile):
        cols = slice(t * tile, (t + 1) * tile)
        cols_im = slice(size + t * tile, size + (t + 1) * tile)
        y = jnp.concatenate([ys[:, cols], ys[:, cols_im]], axis=0)
        fit = jnp.dot(resp[...], y, preferred_element_type=jnp.float32)
        here = receiver_block == (col0 + t * tile) // RB
        covered = jnp.max(jnp.where(here, listed, 0.0), axis=1, keepdims=True)
        for which, slot, out in ((0, OWN, out_own), (1, MATE, out_mate)):
            weight = covered[which * rows : (which + 1) * rows]
            pair = []
            for c in range(2):
                at = 2 * which + c
                value = record(slot, c, cols).astype(jnp.float32) + fit[at * rows : (at + 1) * rows]
                pair.append((weight * value).astype(jnp.bfloat16))
                out[c, :, cols] = pair[c]
            at = slice(2 * which * rows, (2 * which + 1) * rows)
            ms[at, cols] = pair[0]
            ms[at, cols_im] = pair[1]
            at = slice((2 * which + 1) * rows, (2 * which + 2) * rows)
            ms[at, cols] = pair[1]
            ms[at, cols_im] = -pair[0]

    @pl.loop(0, size // tile)
    def _(t):
        for slot in range(6):

            @pl.when(meets(slot, col0 + t * tile))
            def _(slot=slot):
                one = jnp.where(hits(slot, col0 + t * tile), 1.0, 0.0).astype(jnp.bfloat16)
                cols = pl.ds(pl.multiple_of(t * tile, tile), tile)
                at_shots = lax.dot_general(
                    ms[:, cols], one, across, preferred_element_type=jnp.float32
                )
                for c in range(2):
                    at = c * 6 * rows + slot * rows
                    x = resp[:, at : at + rows].astype(jnp.float32)
                    terms = (x * at_shots).reshape(-1, 8, rows)
                    corrs[c] -= jnp.sum(terms, axis=0)

    total = lax.dot_general(ys[...], ms[...], across, preferred_element_type=jnp.float32)
    if not first:
        total = grad_in[...] + total
    if not last:
        grad_out[...] = total
        corr_out[...] = corrs[...]
        return
    sums[...] = total
    even = side == 0
    orders = (
        (grad_own, (LOW, (LOW_X, MATE), OWN, (MATE, HIGH_X), HIGH)),
        (grad_mate, (LOW_X, (OWN, LOW), MATE, (HIGH, OWN), HIGH_X)),
    )
    for which, (out, order) in enumerate(orders):
        for c in range(2):
            at = slice((2 * which + c) * rows, (2 * which + c + 1) * rows)
            for k, slot in enumerate(order):
                pair = slot if isinstance(slot, tuple) else (slot,)
                value = [sums[s * rows : (s + 1) * rows, at] for s in pair]
                value = value[0] if len(pair) == 1 else jnp.where(even, *value)
                out[c, :, k * rows : (k + 1) * rows] = value.T
    corr = [jnp.sum(jnp.sum(corrs[c], axis=0, keepdims=True), axis=1, keepdims=True) for c in range(2)]
    corr_out[...] = corr[0] * waves[0:1, :] - corr[1] * waves[1:2, :]


def chunk(consts, arrays, layout, carry, off, size, half, stride, rows, band, last):
    info, wave, waves, resp, mask = consts
    first = carry is None
    conf = (rows, size, stride, half, off, band, layout, first, last)
    args = [info, wave, waves, resp, mask, *arrays]
    in_specs = [IN_SMEM, IN_SMEM] + [IN_VMEM] * (len(args) - 2)
    aliases = {}
    if not first:
        if not last:
            aliases = {len(args): 2, len(args) + 1: 3}
        args += list(carry)
        in_specs += [IN_VMEM, IN_VMEM]
    if last:
        sums = [jax.ShapeDtypeStruct((2, rows, band), jnp.float32)] * 2
        sums.append(jax.ShapeDtypeStruct((1, waves.shape[1]), jnp.float32))
    else:
        sums = [jax.ShapeDtypeStruct((6 * rows, 4 * rows), jnp.float32)]
        sums.append(jax.ShapeDtypeStruct((2, 8, rows), jnp.float32))
    out_shape = [jax.ShapeDtypeStruct((2, rows, size), jnp.bfloat16)] * 2 + sums
    return pl.pallas_call(
        functools.partial(chunk_kernel, conf),
        out_shape=out_shape,
        in_specs=in_specs,
        out_specs=[IN_VMEM] * len(out_shape),
        scratch_shapes=[
            pltpu.VMEM((6 * rows, 2 * size), jnp.bfloat16),
            pltpu.VMEM((4 * rows, 2 * size), jnp.bfloat16),
            pltpu.VMEM((6 * rows, 4 * rows), jnp.float32),
            pltpu.VMEM((2, 8, rows), jnp.float32),
        ],
        input_output_aliases=aliases,
        compiler_params=PARAMS,
        cost_estimate=LIGHT,
        name="residual_chunk",
    )(*args)


def total_over(value, axis, steps):
    size = lax.axis_size(axis)
    for step in steps:
        value = value + lax.ppermute(value, axis, [(i, i ^ step) for i in range(size)])
    return value


def after(value, *others):
    others = [a for a in others if a is not None]
    return lax.optimization_barrier((value, *others))[0] if others else value


def on_device(data, primaries, wavelet, cover_ids, cover_counts):
    record = data[0]
    _, rows, width = record.shape
    band = primaries.shape[3]
    shots, freqs = lax.axis_size("shot"), lax.axis_size("freq")
    shot_count = shots * rows
    stride = width // shot_count
    half = width // 2
    position = lax.axis_index("shot").astype(jnp.int32)
    freq_index = lax.axis_index("freq").astype(jnp.int32)
    info = jnp.stack([position % 2, position])
    cuts, off = [], 0
    for part in PARTS:
        size = part * (half // sum(PARTS))
        cuts.append((off, size))
        off += size
    steps = len(cuts)

    def swap(a):
        return lax.ppermute(a, "shot", [(s, s ^ 1) for s in range(shots)])

    def neighbours(a):
        return [
            lax.ppermute(a, "shot", [(s, s + d) for s in range(shots) if 0 <= s + d < shots])
            for d in (2, -2)
        ]

    swapped = []
    for n, group in enumerate(GROUPS):
        off, size = cuts[group[0]][0], sum(cuts[m][1] for m in group)
        piece = split(info, record, half, off, size, True)
        swapped.append(swap(after(piece, *swapped[n - 2 : n - 1]) if n >= 2 else piece))
    mine = split(info, record, half, *cuts[0], False)
    near = neighbours(mine)

    listed = jnp.arange(cover_ids.shape[1], dtype=jnp.int32)[None, :] < cover_counts[:, None]
    ids = jnp.arange(width // RB, dtype=jnp.int32)
    covered = jnp.any((cover_ids[:, :, None] == ids) & listed[:, :, None], axis=1)
    covered = jnp.pad(covered.T.astype(jnp.bfloat16), ((0, 0), (0, band - rows)))
    params = jnp.concatenate([primaries[0].reshape(2 * rows, band), covered], axis=0)
    params_there = swap(after(params, swapped[0]))
    resp, mask = prepare(info, params, params_there, rows)
    times = jnp.arange(NT, dtype=jnp.int32).astype(jnp.float32)
    phase = 2.0 * math.pi * (freq_index + 1).astype(jnp.float32) * times / NT
    scale = 1.0 / math.sqrt(shot_count * band)
    waves = jnp.stack([jnp.cos(phase), jnp.sin(phase)]) * scale
    consts = (info, wavelet[0], waves, resp, mask)

    far = neighbours(swapped[0])
    arrays = [near[0], far[0], mine, swapped[0], near[1], far[1]]
    layout = tuple((n, None) for n in range(6))
    both = [None]
    carry = whole = None
    sent = []
    for n, (off, size) in enumerate(cuts):
        if n + 1 < steps:
            if n + 1 == len(both):
                group = GROUPS[n + 1]
                both += join(info, record, swapped[n + 1], half, [cuts[m] for m in group])
            ahead = neighbours(both[n + 1])
        gate = list(both[n + 1 : n + 2])
        if n >= 2:
            here, back, at = sent[n - 2]
            whole = place(info, here, back, whole, half, at)
            info_now, whole = lax.optimization_barrier((info, whole, *gate))[:2]
        else:
            info_now = after(info, *gate)
        here, there, *grad, corr = chunk(
            (info_now, *consts[1:]),
            arrays, layout, carry, off, size, half, stride, rows, band, n == steps - 1,
        )
        carry = (grad[0], corr)
        sent.append((here, swap(there), off))
        if n + 1 < steps:
            arrays = [both[n + 1], *ahead]
            layout = ((1, 0), (1, 1), (0, 0), (0, 1), (2, 0), (2, 1))
    for here, back, at in sent[-2:]:
        whole = place(info, here, back, whole, half, at)
    gradient = grad[0] + swap(grad[1])
    if shots & (shots - 1) or freqs & (freqs - 1):
        total = lax.psum(corr, ("shot", "freq"))
    else:
        total = total_over(corr, "shot", [2**i for i in range(1, shots.bit_length() - 1)])
        total = total_over(total, "freq", [2**i for i in range(freqs.bit_length() - 1)])
        total = total_over(total, "shot", [1])
    return (whole[None], gradient[None], total[0])


def solution(mesh):
    in_specs = (
        P("freq", None, "shot", None),
        P("freq", None, "shot", None),
        P("freq", None),
        P("shot", None),
        P("shot"),
    )
    out_specs = (P("freq", None, "shot", None), P("freq", None, "shot", None), P())
    return jax.shard_map(
        on_device, mesh=mesh, in_specs=in_specs, out_specs=out_specs, check_vma=False
    )
```

```python
import functools
import math

import jax
import jax.numpy as jnp
from jax import lax
from jax.experimental import pallas as pl
from jax.experimental.pallas import tpu as pltpu
from jax.sharding import PartitionSpec as P

RB = 512
NT = 128
VMEM = 14 * 1024 * 1024
PARTS = (4, 4, 4, 2, 2)
GROUPS = ((0,), (1,), (2,), (3, 4))
LOW, LOW_X, OWN, MATE, HIGH, HIGH_X = range(6)
IN_SMEM = pl.BlockSpec(memory_space=pltpu.SMEM)
IN_VMEM = pl.BlockSpec(memory_space=pltpu.VMEM)
IN_HBM = pl.BlockSpec(memory_space=pltpu.HBM)
PARAMS = pltpu.CompilerParams(vmem_limit_bytes=VMEM)
LIGHT = pl.CostEstimate(flops=0, bytes_accessed=0, transcendentals=0)


def columns(ref, start, size):
    return ref.at[:, :, pl.ds(pl.multiple_of(start, 128), size)]


def run(copies):
    for copy in copies:
        copy.start()
    for copy in copies:
        copy.wait()


def split_kernel(half, off, size, other, info, whole, out, sem):
    side = 1 - info[0] if other else info[0]
    run([pltpu.make_async_copy(columns(whole, side * half + off, size), out, sem)])


def split(info, whole, half, off, size, other):
    return pl.pallas_call(
        functools.partial(split_kernel, half, off, size, other),
        out_shape=jax.ShapeDtypeStruct((*whole.shape[:2], size), whole.dtype),
        in_specs=[IN_SMEM, IN_HBM],
        out_specs=IN_VMEM,
        scratch_shapes=[pltpu.SemaphoreType.DMA],
        compiler_params=PARAMS,
        cost_estimate=LIGHT,
        name="split_columns",
    )(info, whole)


def join_kernel(half, cuts, info, whole, theirs, *refs):
    outs, sems = refs[:-1], refs[-1]
    base = cuts[0][0]
    copies = []
    for n, (off, size) in enumerate(cuts):
        mine = columns(whole, info[0] * half + off, size)
        copies.append(pltpu.make_async_copy(mine, outs[n].at[0], sems.at[2 * n]))
        got = theirs.at[:, :, pl.ds(off - base, size)]
        copies.append(pltpu.make_async_copy(got, outs[n].at[1], sems.at[2 * n + 1]))
    run(copies)


def join(info, whole, theirs, half, cuts):
    return pl.pallas_call(
        functools.partial(join_kernel, half, cuts),
        out_shape=[
            jax.ShapeDtypeStruct((2, *theirs.shape[:2], size), theirs.dtype) for _, size in cuts
        ],
        in_specs=[IN_SMEM, IN_HBM, IN_VMEM],
        out_specs=[IN_VMEM] * len(cuts),
        scratch_shapes=[pltpu.SemaphoreType.DMA((2 * len(cuts),))],
        compiler_params=PARAMS,
        cost_estimate=LIGHT,
        name="join_blocks",
    )(info, whole, theirs)


def place_kernel(half, off, size, info, here, there, *refs):
    whole, sems = refs[-2:]
    side = info[0]
    run(
        [
            pltpu.make_async_copy(here, columns(whole, side * half + off, size), sems.at[0]),
            pltpu.make_async_copy(there, columns(whole, (1 - side) * half + off, size), sems.at[1]),
        ]
    )


def place(info, here, there, whole, half, off):
    _, rows, size = here.shape
    first = whole is None
    return pl.pallas_call(
        functools.partial(place_kernel, half, off, size),
        out_shape=jax.ShapeDtypeStruct((2, rows, 2 * half), here.dtype),
        in_specs=[IN_SMEM, IN_VMEM, IN_VMEM] + ([] if first else [IN_HBM]),
        out_specs=IN_HBM,
        scratch_shapes=[pltpu.SemaphoreType.DMA((2,))],
        input_output_aliases={} if first else {3: 0},
        compiler_params=PARAMS,
        cost_estimate=LIGHT,
        name="place_columns",
    )(info, here, there, *([] if first else [whole]))


def prepare_kernel(info, own, mate, resp, mask):
    rows = mask.shape[0] // 2
    none = None
    tables = (
        ((0, 1, 2, 3, 4, none), (none, 0, 1, 2, 3, 4)),
        ((0, none, 2, 1, 4, 3), (1, 0, 3, 2, none, 4)),
    )
    for which, params in ((0, own), (1, mate)):
        mask[which * rows : (which + 1) * rows, :] = params[2 * rows :, :rows].astype(jnp.float32).T
        line = slice(2 * which * rows, (2 * which + 1) * rows)
        line_im = slice((2 * which + 1) * rows, (2 * which + 2) * rows)
        for side in range(2):

            @pl.when(info[0] == side)
            def _(params=params, line=line, line_im=line_im, table=tables[side][which]):
                for slot, k in enumerate(table):
                    at = slice(slot * rows, (slot + 1) * rows)
                    at_im = slice((6 + slot) * rows, (7 + slot) * rows)
                    if k is None:
                        re = im = jnp.zeros((rows, rows), resp.dtype)
                    else:
                        re = params[:rows, k * rows : (k + 1) * rows]
                        im = params[rows : 2 * rows, k * rows : (k + 1) * rows]
                    resp[line, at] = re
                    resp[line, at_im] = -im
                    resp[line_im, at] = im
                    resp[line_im, at_im] = re


def prepare(info, own, mate, rows):
    blocks = own.shape[0] - 2 * rows
    return pl.pallas_call(
        prepare_kernel,
        out_shape=[
            jax.ShapeDtypeStruct((4 * rows, 12 * rows), own.dtype),
            jax.ShapeDtypeStruct((2 * rows, blocks), jnp.float32),
        ],
        in_specs=[IN_SMEM, IN_VMEM, IN_VMEM],
        out_specs=[IN_VMEM, IN_VMEM],
        compiler_params=PARAMS,
        cost_estimate=LIGHT,
        name="prepare_response",
    )(info, own, mate)


def chunk_kernel(conf, *refs):
    rows, size, stride, half, off, scale, layout, first, last = conf
    refs = list(refs)
    info, wave, resp, mask = (refs.pop(0) for _ in range(4))
    given = [refs.pop(0) for _ in range(max(ref for ref, _ in layout) + 1)]
    if not first:
        grad_in, corr_in = refs.pop(0), refs.pop(0)
    out_own, out_mate = refs.pop(0), refs.pop(0)
    if last:
        grad_own, grad_mate, corr_out = (refs.pop(0) for _ in range(3))
    else:
        grad_out, corr_out = refs.pop(0), refs.pop(0)
    ys, ms, sums, corrs = refs
    side, pos = info[0], info[1]
    even = side == 0
    col0 = side * half + off
    tile = RB if (off | size) % RB == 0 else RB // 2

    def record(slot, c, cols=slice(None)):
        ref, part = layout[slot]
        return given[ref][c, :, cols] if part is None else given[ref][part, c, :, cols]

    piece = min(RB // 2, rows * stride)

    def hit_slot(start):
        ahead = start // (rows * stride) - (pos - side - 2)
        inside = (ahead >= 0) & (ahead < 6)
        return inside, jnp.where(even, ahead, ahead + 1 - 2 * lax.rem(ahead, 2))

    def hits(start):
        shots = lax.broadcasted_iota(jnp.int32, (rows, piece), 0)
        cols = lax.rem(start, rows * stride) + lax.broadcasted_iota(jnp.int32, (rows, piece), 1)
        return shots * stride == cols

    for slot in range(6):
        at = slice(slot * rows, (slot + 1) * rows)
        for c in range(2):
            ys[at, c * size : (c + 1) * size] = record(slot, c)

    @pl.loop(0, size // piece)
    def _(t):
        inside, slot = hit_slot(col0 + t * piece)

        @pl.when(inside)
        def _():
            hit = hits(col0 + t * piece)
            at = pl.ds(pl.multiple_of(slot * rows, rows), rows)
            for c in range(2):
                cols = pl.ds(pl.multiple_of(c * size + t * piece, piece), piece)
                direct = jnp.where(hit, wave[c], 0.0)
                ys[at, cols] = (ys[at, cols].astype(jnp.float32) - direct).astype(jnp.bfloat16)

    across = (((1,), (1,)), ((), ()))
    corrs[...] = jnp.zeros_like(corrs) if first else corr_in[...]
    listed = mask[...]
    receiver_block = lax.broadcasted_iota(jnp.int32, listed.shape, 1)
    for t in range(size // tile):
        cols = slice(t * tile, (t + 1) * tile)
        cols_im = slice(size + t * tile, size + (t + 1) * tile)
        y = jnp.concatenate([ys[:, cols], ys[:, cols_im]], axis=0)
        fit = jnp.dot(resp[...], y, preferred_element_type=jnp.float32)
        here = receiver_block == (col0 + t * tile) // RB
        covered = jnp.max(jnp.where(here, listed, 0.0), axis=1, keepdims=True)
        for which, slot, out in ((0, OWN, out_own), (1, MATE, out_mate)):
            weight = covered[which * rows : (which + 1) * rows]
            pair = []
            for c in range(2):
                at = 2 * which + c
                value = record(slot, c, cols).astype(jnp.float32) + fit[at * rows : (at + 1) * rows]
                pair.append((weight * value).astype(jnp.bfloat16))
                out[c, :, cols] = pair[c]
            at = slice(2 * which * rows, (2 * which + 1) * rows)
            ms[at, cols] = pair[0]
            ms[at, cols_im] = pair[1]
            at = slice((2 * which + 1) * rows, (2 * which + 2) * rows)
            ms[at, cols] = pair[1]
            ms[at, cols_im] = -pair[0]

    @pl.loop(0, size // piece)
    def _(t):
        inside, slot = hit_slot(col0 + t * piece)

        @pl.when(inside)
        def _():
            one = jnp.where(hits(col0 + t * piece), 1.0, 0.0).astype(jnp.bfloat16)
            cols = pl.ds(pl.multiple_of(t * piece, piece), piece)
            at_shots = lax.dot_general(ms[:, cols], one, across, preferred_element_type=jnp.float32)
            for c in range(2):
                at = pl.ds(pl.multiple_of((c * 6 + slot) * rows, rows), rows)
                terms = (resp[:, at].astype(jnp.float32) * at_shots).reshape(-1, 8, rows)
                corrs[c] -= jnp.sum(terms, axis=0)

    total = lax.dot_general(ys[...], ms[...], across, preferred_element_type=jnp.float32)
    if not first:
        total = grad_in[...] + total
    if not last:
        grad_out[...] = total
        corr_out[...] = corrs[...]
        return
    sums[...] = total
    orders = (
        (grad_own, (LOW, (LOW_X, MATE), OWN, (MATE, HIGH_X), HIGH)),
        (grad_mate, (LOW_X, (OWN, LOW), MATE, (HIGH, OWN), HIGH_X)),
    )
    for which, (out, order) in enumerate(orders):
        for c in range(2):
            at = slice((2 * which + c) * rows, (2 * which + c + 1) * rows)
            for k, slot in enumerate(order):
                pair = slot if isinstance(slot, tuple) else (slot,)
                value = [sums[s * rows : (s + 1) * rows, at] for s in pair]
                value = value[0] if len(pair) == 1 else jnp.where(even, *value)
                out[c, :, k * rows : (k + 1) * rows] = value.T
    corr = [jnp.sum(jnp.sum(corrs[c], axis=0, keepdims=True), axis=1, keepdims=True) for c in range(2)]
    turns = lax.rem((info[2] + 1) * lax.broadcasted_iota(jnp.int32, (1, NT), 1), NT)
    phase = turns.astype(jnp.float32) * (2.0 * math.pi / NT)
    corr_out[...] = (corr[0] * jnp.cos(phase) - corr[1] * jnp.sin(phase)) * scale


def chunk(consts, arrays, layout, carry, off, size, half, stride, rows, band, last):
    info, wave, resp, mask = consts
    first = carry is None
    scale = 1.0 / math.sqrt(2 * half // stride * band)
    conf = (rows, size, stride, half, off, scale, layout, first, last)
    args = [info, wave, resp, mask, *arrays]
    in_specs = [IN_SMEM, IN_SMEM] + [IN_VMEM] * (len(args) - 2)
    aliases = {}
    if not first:
        if not last:
            aliases = {len(args): 2, len(args) + 1: 3}
        args += list(carry)
        in_specs += [IN_VMEM, IN_VMEM]
    if last:
        sums = [jax.ShapeDtypeStruct((2, rows, band), jnp.float32)] * 2
        sums.append(jax.ShapeDtypeStruct((1, NT), jnp.float32))
    else:
        sums = [jax.ShapeDtypeStruct((6 * rows, 4 * rows), jnp.float32)]
        sums.append(jax.ShapeDtypeStruct((2, 8, rows), jnp.float32))
    out_shape = [jax.ShapeDtypeStruct((2, rows, size), jnp.bfloat16)] * 2 + sums
    return pl.pallas_call(
        functools.partial(chunk_kernel, conf),
        out_shape=out_shape,
        in_specs=in_specs,
        out_specs=[IN_VMEM] * len(out_shape),
        scratch_shapes=[
            pltpu.VMEM((6 * rows, 2 * size), jnp.bfloat16),
            pltpu.VMEM((4 * rows, 2 * size), jnp.bfloat16),
            pltpu.VMEM((6 * rows, 4 * rows), jnp.float32),
            pltpu.VMEM((2, 8, rows), jnp.float32),
        ],
        input_output_aliases=aliases,
        compiler_params=PARAMS,
        cost_estimate=LIGHT,
        name="residual_chunk",
    )(*args)


def total_over(value, axis, steps):
    size = lax.axis_size(axis)
    for step in steps:
        value = value + lax.ppermute(value, axis, [(i, i ^ step) for i in range(size)])
    return value


def after(value, *others):
    others = [a for a in others if a is not None]
    return lax.optimization_barrier((value, *others))[0] if others else value


def on_device(data, primaries, wavelet, cover_ids, cover_counts):
    record = data[0]
    _, rows, width = record.shape
    band = primaries.shape[3]
    shots, freqs = lax.axis_size("shot"), lax.axis_size("freq")
    shot_count = shots * rows
    stride = width // shot_count
    half = width // 2
    position = lax.axis_index("shot").astype(jnp.int32)
    freq_index = lax.axis_index("freq").astype(jnp.int32)
    info = jnp.stack([position % 2, position, freq_index])
    cuts, off = [], 0
    for part in PARTS:
        size = part * (half // sum(PARTS))
        cuts.append((off, size))
        off += size
    steps = len(cuts)

    def swap(a):
        return lax.ppermute(a, "shot", [(s, s ^ 1) for s in range(shots)])

    def neighbours(a):
        return [
            lax.ppermute(a, "shot", [(s, s + d) for s in range(shots) if 0 <= s + d < shots])
            for d in (2, -2)
        ]

    swapped = []
    for n, group in enumerate(GROUPS):
        off, size = cuts[group[0]][0], sum(cuts[m][1] for m in group)
        piece = split(info, record, half, off, size, True)
        swapped.append(swap(after(piece, *swapped[n - 2 : n - 1]) if n >= 2 else piece))
    mine = split(info, record, half, *cuts[0], False)
    near = neighbours(mine)

    listed = jnp.arange(cover_ids.shape[1], dtype=jnp.int32)[None, :] < cover_counts[:, None]
    ids = jnp.arange(width // RB, dtype=jnp.int32)
    covered = jnp.any((cover_ids[:, :, None] == ids) & listed[:, :, None], axis=1)
    covered = jnp.pad(covered.T.astype(jnp.bfloat16), ((0, 0), (0, band - rows)))
    params = jnp.concatenate([primaries[0].reshape(2 * rows, band), covered], axis=0)
    params_there = swap(after(params, swapped[0]))
    resp, mask = prepare(info, params, params_there, rows)
    consts = (info, wavelet[0], resp, mask)

    far = neighbours(swapped[0])
    arrays = [near[0], far[0], mine, swapped[0], near[1], far[1]]
    layout = tuple((n, None) for n in range(6))
    both = [None]
    carry = whole = None
    sent = []
    for n, (off, size) in enumerate(cuts):
        if n + 1 < steps:
            if n + 1 == len(both):
                group = GROUPS[n + 1]
                both += join(info, record, swapped[n + 1], half, [cuts[m] for m in group])
            ahead = neighbours(both[n + 1])
        gate = list(both[n + 1 : n + 2])
        if n >= 2:
            here, back, at = sent[n - 2]
            whole = place(info, here, back, whole, half, at)
            info_now, whole = lax.optimization_barrier((info, whole, *gate))[:2]
        else:
            info_now = after(info, *gate)
        here, there, *grad, corr = chunk(
            (info_now, *consts[1:]),
            arrays, layout, carry, off, size, half, stride, rows, band, n == steps - 1,
        )
        carry = (grad[0], corr)
        sent.append((here, swap(there), off))
        if n + 1 < steps:
            arrays = [both[n + 1], *ahead]
            layout = ((1, 0), (1, 1), (0, 0), (0, 1), (2, 0), (2, 1))
    for here, back, at in sent[-2:]:
        whole = place(info, here, back, whole, half, at)
    gradient = grad[0] + swap(grad[1])
    if shots & (shots - 1) or freqs & (freqs - 1):
        total = lax.psum(corr, ("shot", "freq"))
    else:
        total = total_over(corr, "shot", [2**i for i in range(1, shots.bit_length() - 1)])
        total = total_over(total, "freq", [2**i for i in range(freqs.bit_length() - 1)])
        total = total_over(total, "shot", [1])
    return (whole[None], gradient[None], total[0])


def solution(mesh):
    in_specs = (
        P("freq", None, "shot", None),
        P("freq", None, "shot", None),
        P("freq", None),
        P("shot", None),
        P("shot"),
    )
    out_specs = (P("freq", None, "shot", None), P("freq", None, "shot", None), P())
    return jax.shard_map(
        on_device, mesh=mesh, in_specs=in_specs, out_specs=out_specs, check_vma=False
    )
```

```python
import functools
import math

import jax
import jax.numpy as jnp
from jax import lax
from jax.experimental import pallas as pl
from jax.experimental.pallas import tpu as pltpu
from jax.sharding import PartitionSpec as P

RB = 512
NT = 128
VMEM = 14 * 1024 * 1024
PARTS = (7, 4, 4, 1)
GROUPS = ((0,), (1,), (2, 3))
LOW, LOW_X, OWN, MATE, HIGH, HIGH_X = range(6)
IN_SMEM = pl.BlockSpec(memory_space=pltpu.SMEM)
IN_VMEM = pl.BlockSpec(memory_space=pltpu.VMEM)
IN_HBM = pl.BlockSpec(memory_space=pltpu.HBM)
PARAMS = pltpu.CompilerParams(vmem_limit_bytes=VMEM)
LIGHT = pl.CostEstimate(flops=0, bytes_accessed=0, transcendentals=0)


def columns(ref, start, size):
    return ref.at[:, :, pl.ds(pl.multiple_of(start, 128), size)]


def run(copies):
    for copy in copies:
        copy.start()
    for copy in copies:
        copy.wait()


def split_kernel(half, off, size, other, info, whole, out, sem):
    side = 1 - info[0] if other else info[0]
    run([pltpu.make_async_copy(columns(whole, side * half + off, size), out, sem)])


def split(info, whole, half, off, size, other):
    return pl.pallas_call(
        functools.partial(split_kernel, half, off, size, other),
        out_shape=jax.ShapeDtypeStruct((*whole.shape[:2], size), whole.dtype),
        in_specs=[IN_SMEM, IN_HBM],
        out_specs=IN_VMEM,
        scratch_shapes=[pltpu.SemaphoreType.DMA],
        compiler_params=PARAMS,
        cost_estimate=LIGHT,
        name="split_columns",
    )(info, whole)


def join_kernel(half, cuts, info, whole, theirs, *refs):
    outs, sems = refs[:-1], refs[-1]
    base = cuts[0][0]
    copies = []
    for n, (off, size) in enumerate(cuts):
        mine = columns(whole, info[0] * half + off, size)
        copies.append(pltpu.make_async_copy(mine, outs[n].at[0], sems.at[2 * n]))
        got = theirs.at[:, :, pl.ds(off - base, size)]
        copies.append(pltpu.make_async_copy(got, outs[n].at[1], sems.at[2 * n + 1]))
    run(copies)


def join(info, whole, theirs, half, cuts):
    return pl.pallas_call(
        functools.partial(join_kernel, half, cuts),
        out_shape=[
            jax.ShapeDtypeStruct((2, *theirs.shape[:2], size), theirs.dtype) for _, size in cuts
        ],
        in_specs=[IN_SMEM, IN_HBM, IN_VMEM],
        out_specs=[IN_VMEM] * len(cuts),
        scratch_shapes=[pltpu.SemaphoreType.DMA((2 * len(cuts),))],
        compiler_params=PARAMS,
        cost_estimate=LIGHT,
        name="join_blocks",
    )(info, whole, theirs)


def place_kernel(half, off, size, info, here, there, *refs):
    whole, sems = refs[-2:]
    side = info[0]
    run(
        [
            pltpu.make_async_copy(here, columns(whole, side * half + off, size), sems.at[0]),
            pltpu.make_async_copy(there, columns(whole, (1 - side) * half + off, size), sems.at[1]),
        ]
    )


def place(info, here, there, whole, half, off):
    _, rows, size = here.shape
    first = whole is None
    return pl.pallas_call(
        functools.partial(place_kernel, half, off, size),
        out_shape=jax.ShapeDtypeStruct((2, rows, 2 * half), here.dtype),
        in_specs=[IN_SMEM, IN_VMEM, IN_VMEM] + ([] if first else [IN_HBM]),
        out_specs=IN_HBM,
        scratch_shapes=[pltpu.SemaphoreType.DMA((2,))],
        input_output_aliases={} if first else {3: 0},
        compiler_params=PARAMS,
        cost_estimate=LIGHT,
        name="place_columns",
    )(info, here, there, *([] if first else [whole]))


def prepare_kernel(info, own, mate, resp, mask):
    rows = mask.shape[0] // 2
    none = None
    tables = (
        ((0, 1, 2, 3, 4, none), (none, 0, 1, 2, 3, 4)),
        ((0, none, 2, 1, 4, 3), (1, 0, 3, 2, none, 4)),
    )
    for which, params in ((0, own), (1, mate)):
        mask[which * rows : (which + 1) * rows, :] = params[2 * rows :, :rows].astype(jnp.float32).T
        line = slice(2 * which * rows, (2 * which + 1) * rows)
        line_im = slice((2 * which + 1) * rows, (2 * which + 2) * rows)
        for side in range(2):

            @pl.when(info[0] == side)
            def _(params=params, line=line, line_im=line_im, table=tables[side][which]):
                for slot, k in enumerate(table):
                    at = slice(slot * rows, (slot + 1) * rows)
                    at_im = slice((6 + slot) * rows, (7 + slot) * rows)
                    if k is None:
                        re = im = jnp.zeros((rows, rows), resp.dtype)
                    else:
                        re = params[:rows, k * rows : (k + 1) * rows]
                        im = params[rows : 2 * rows, k * rows : (k + 1) * rows]
                    resp[line, at] = re
                    resp[line, at_im] = -im
                    resp[line_im, at] = im
                    resp[line_im, at_im] = re


def prepare(info, own, mate, rows):
    blocks = own.shape[0] - 2 * rows
    return pl.pallas_call(
        prepare_kernel,
        out_shape=[
            jax.ShapeDtypeStruct((4 * rows, 12 * rows), own.dtype),
            jax.ShapeDtypeStruct((2 * rows, blocks), jnp.float32),
        ],
        in_specs=[IN_SMEM, IN_VMEM, IN_VMEM],
        out_specs=[IN_VMEM, IN_VMEM],
        compiler_params=PARAMS,
        cost_estimate=LIGHT,
        name="prepare_response",
    )(info, own, mate)


def chunk_kernel(conf, *refs):
    rows, size, stride, half, off, scale, layout, first, last = conf
    refs = list(refs)
    info, wave, resp, mask = (refs.pop(0) for _ in range(4))
    given = [refs.pop(0) for _ in range(max(ref for ref, _ in layout) + 1)]
    if not first:
        grad_in, corr_in = refs.pop(0), refs.pop(0)
    out_own, out_mate = refs.pop(0), refs.pop(0)
    if last:
        grad_own, grad_mate, corr_out = (refs.pop(0) for _ in range(3))
    else:
        grad_out, corr_out = refs.pop(0), refs.pop(0)
    ys, ms, sums, corrs = refs
    side, pos = info[0], info[1]
    even = side == 0
    col0 = side * half + off
    spans, at = [], 0
    while at < size:
        wide = RB if (off + at) % RB == 0 and at + RB <= size else RB // 2
        spans.append((at, at + wide))
        at += wide

    def record(slot, c, cols=slice(None)):
        ref, part = layout[slot]
        return given[ref][c, :, cols] if part is None else given[ref][part, c, :, cols]

    piece = min(RB // 2, rows * stride)

    def hit_slot(start):
        ahead = start // (rows * stride) - (pos - side - 2)
        inside = (ahead >= 0) & (ahead < 6)
        return inside, jnp.where(even, ahead, ahead + 1 - 2 * lax.rem(ahead, 2))

    def hits(start):
        shots = lax.broadcasted_iota(jnp.int32, (rows, piece), 0)
        cols = lax.rem(start, rows * stride) + lax.broadcasted_iota(jnp.int32, (rows, piece), 1)
        return shots * stride == cols

    for slot in range(6):
        at = slice(slot * rows, (slot + 1) * rows)
        for c in range(2):
            ys[at, c * size : (c + 1) * size] = record(slot, c)

    @pl.loop(0, size // piece)
    def _(t):
        inside, slot = hit_slot(col0 + t * piece)

        @pl.when(inside)
        def _():
            hit = hits(col0 + t * piece)
            at = pl.ds(pl.multiple_of(slot * rows, rows), rows)
            for c in range(2):
                cols = pl.ds(pl.multiple_of(c * size + t * piece, piece), piece)
                direct = jnp.where(hit, wave[c], 0.0)
                ys[at, cols] = (ys[at, cols].astype(jnp.float32) - direct).astype(jnp.bfloat16)

    across = (((1,), (1,)), ((), ()))
    corrs[...] = jnp.zeros_like(corrs) if first else corr_in[...]
    listed = mask[...]
    receiver_block = lax.broadcasted_iota(jnp.int32, listed.shape, 1)
    for low, high in spans:
        cols = slice(low, high)
        cols_im = slice(size + low, size + high)
        y = jnp.concatenate([ys[:, cols], ys[:, cols_im]], axis=0)
        fit = jnp.dot(resp[...], y, preferred_element_type=jnp.float32)
        here = receiver_block == (col0 + low) // RB
        covered = jnp.max(jnp.where(here, listed, 0.0), axis=1, keepdims=True)
        for which, slot, out in ((0, OWN, out_own), (1, MATE, out_mate)):
            weight = covered[which * rows : (which + 1) * rows]
            pair = []
            for c in range(2):
                at = 2 * which + c
                value = record(slot, c, cols).astype(jnp.float32) + fit[at * rows : (at + 1) * rows]
                pair.append((weight * value).astype(jnp.bfloat16))
                out[c, :, cols] = pair[c]
            at = slice(2 * which * rows, (2 * which + 1) * rows)
            ms[at, cols] = pair[0]
            ms[at, cols_im] = pair[1]
            at = slice((2 * which + 1) * rows, (2 * which + 2) * rows)
            ms[at, cols] = pair[1]
            ms[at, cols_im] = -pair[0]

    @pl.loop(0, size // piece)
    def _(t):
        inside, slot = hit_slot(col0 + t * piece)

        @pl.when(inside)
        def _():
            one = jnp.where(hits(col0 + t * piece), 1.0, 0.0).astype(jnp.bfloat16)
            cols = pl.ds(pl.multiple_of(t * piece, piece), piece)
            at_shots = lax.dot_general(ms[:, cols], one, across, preferred_element_type=jnp.float32)
            for c in range(2):
                at = pl.ds(pl.multiple_of((c * 6 + slot) * rows, rows), rows)
                terms = (resp[:, at].astype(jnp.float32) * at_shots).reshape(-1, 8, rows)
                corrs[c] -= jnp.sum(terms, axis=0)

    total = lax.dot_general(ys[...], ms[...], across, preferred_element_type=jnp.float32)
    if not first:
        total = grad_in[...] + total
    if not last:
        grad_out[...] = total
        corr_out[...] = corrs[...]
        return
    sums[...] = total
    orders = (
        (grad_own, (LOW, (LOW_X, MATE), OWN, (MATE, HIGH_X), HIGH)),
        (grad_mate, (LOW_X, (OWN, LOW), MATE, (HIGH, OWN), HIGH_X)),
    )
    for which, (out, order) in enumerate(orders):
        for c in range(2):
            at = slice((2 * which + c) * rows, (2 * which + c + 1) * rows)
            for k, slot in enumerate(order):
                pair = slot if isinstance(slot, tuple) else (slot,)
                value = [sums[s * rows : (s + 1) * rows, at] for s in pair]
                value = value[0] if len(pair) == 1 else jnp.where(even, *value)
                out[c, :, k * rows : (k + 1) * rows] = value.T
    corr = [jnp.sum(jnp.sum(corrs[c], axis=0, keepdims=True), axis=1, keepdims=True) for c in range(2)]
    turns = lax.rem((info[2] + 1) * lax.broadcasted_iota(jnp.int32, (1, NT), 1), NT)
    phase = turns.astype(jnp.float32) * (2.0 * math.pi / NT)
    corr_out[...] = (corr[0] * jnp.cos(phase) - corr[1] * jnp.sin(phase)) * scale


def chunk(consts, arrays, layout, carry, off, size, half, stride, rows, band, last):
    info, wave, resp, mask = consts
    first = carry is None
    scale = 1.0 / math.sqrt(2 * half // stride * band)
    conf = (rows, size, stride, half, off, scale, layout, first, last)
    args = [info, wave, resp, mask, *arrays]
    in_specs = [IN_SMEM, IN_SMEM] + [IN_VMEM] * (len(args) - 2)
    aliases = {}
    if not first:
        if not last:
            aliases = {len(args): 2, len(args) + 1: 3}
        args += list(carry)
        in_specs += [IN_VMEM, IN_VMEM]
    if last:
        sums = [jax.ShapeDtypeStruct((2, rows, band), jnp.float32)] * 2
        sums.append(jax.ShapeDtypeStruct((1, NT), jnp.float32))
    else:
        sums = [jax.ShapeDtypeStruct((6 * rows, 4 * rows), jnp.float32)]
        sums.append(jax.ShapeDtypeStruct((2, 8, rows), jnp.float32))
    out_shape = [jax.ShapeDtypeStruct((2, rows, size), jnp.bfloat16)] * 2 + sums
    return pl.pallas_call(
        functools.partial(chunk_kernel, conf),
        out_shape=out_shape,
        in_specs=in_specs,
        out_specs=[IN_VMEM] * len(out_shape),
        scratch_shapes=[
            pltpu.VMEM((6 * rows, 2 * size), jnp.bfloat16),
            pltpu.VMEM((4 * rows, 2 * size), jnp.bfloat16),
            pltpu.VMEM((6 * rows, 4 * rows), jnp.float32),
            pltpu.VMEM((2, 8, rows), jnp.float32),
        ],
        input_output_aliases=aliases,
        compiler_params=PARAMS,
        cost_estimate=LIGHT,
        name="residual_chunk",
    )(*args)


def total_over(value, axis, steps):
    size = lax.axis_size(axis)
    for step in steps:
        value = value + lax.ppermute(value, axis, [(i, i ^ step) for i in range(size)])
    return value


def after(value, *others):
    others = [a for a in others if a is not None]
    return lax.optimization_barrier((value, *others))[0] if others else value


def on_device(data, primaries, wavelet, cover_ids, cover_counts):
    record = data[0]
    _, rows, width = record.shape
    band = primaries.shape[3]
    shots, freqs = lax.axis_size("shot"), lax.axis_size("freq")
    shot_count = shots * rows
    stride = width // shot_count
    half = width // 2
    position = lax.axis_index("shot").astype(jnp.int32)
    freq_index = lax.axis_index("freq").astype(jnp.int32)
    info = jnp.stack([position % 2, position, freq_index])
    cuts, off = [], 0
    for part in PARTS:
        size = part * (half // sum(PARTS))
        cuts.append((off, size))
        off += size
    steps = len(cuts)

    def swap(a):
        return lax.ppermute(a, "shot", [(s, s ^ 1) for s in range(shots)])

    def neighbours(a):
        return [
            lax.ppermute(a, "shot", [(s, s + d) for s in range(shots) if 0 <= s + d < shots])
            for d in (2, -2)
        ]

    swapped = []
    for n, group in enumerate(GROUPS):
        off, size = cuts[group[0]][0], sum(cuts[m][1] for m in group)
        piece = split(info, record, half, off, size, True)
        swapped.append(swap(after(piece, *swapped[n - 2 : n - 1]) if n >= 2 else piece))
    mine = split(info, record, half, *cuts[0], False)
    near = neighbours(mine)

    listed = jnp.arange(cover_ids.shape[1], dtype=jnp.int32)[None, :] < cover_counts[:, None]
    ids = jnp.arange(width // RB, dtype=jnp.int32)
    covered = jnp.any((cover_ids[:, :, None] == ids) & listed[:, :, None], axis=1)
    covered = jnp.pad(covered.T.astype(jnp.bfloat16), ((0, 0), (0, band - rows)))
    params = jnp.concatenate([primaries[0].reshape(2 * rows, band), covered], axis=0)
    params_there = swap(after(params, swapped[0]))
    resp, mask = prepare(info, params, params_there, rows)
    consts = (info, wavelet[0], resp, mask)

    far = neighbours(swapped[0])
    arrays = [near[0], far[0], mine, swapped[0], near[1], far[1]]
    layout = tuple((n, None) for n in range(6))
    both = [None]
    carry = whole = None
    sent = []
    for n, (off, size) in enumerate(cuts):
        if n + 1 < steps:
            if n + 1 == len(both):
                group = GROUPS[n + 1]
                both += join(info, record, swapped[n + 1], half, [cuts[m] for m in group])
            ahead = neighbours(both[n + 1])
        gate = list(both[n + 1 : n + 2])
        if n >= 2:
            here, back, at = sent[n - 2]
            whole = place(info, here, back, whole, half, at)
            info_now, whole = lax.optimization_barrier((info, whole, *gate))[:2]
        else:
            info_now = after(info, *gate)
        here, there, *grad, corr = chunk(
            (info_now, *consts[1:]),
            arrays, layout, carry, off, size, half, stride, rows, band, n == steps - 1,
        )
        carry = (grad[0], corr)
        sent.append((here, swap(there), off))
        if n + 1 < steps:
            arrays = [both[n + 1], *ahead]
            layout = ((1, 0), (1, 1), (0, 0), (0, 1), (2, 0), (2, 1))
    for here, back, at in sent[-2:]:
        whole = place(info, here, back, whole, half, at)
    gradient = grad[0] + swap(grad[1])
    if shots & (shots - 1) or freqs & (freqs - 1):
        total = lax.psum(corr, ("shot", "freq"))
    else:
        total = total_over(corr, "shot", [2**i for i in range(1, shots.bit_length() - 1)])
        total = total_over(total, "freq", [2**i for i in range(freqs.bit_length() - 1)])
        total = total_over(total, "shot", [1])
    return (whole[None], gradient[None], total[0])


def solution(mesh):
    in_specs = (
        P("freq", None, "shot", None),
        P("freq", None, "shot", None),
        P("freq", None),
        P("shot", None),
        P("shot"),
    )
    out_specs = (P("freq", None, "shot", None), P("freq", None, "shot", None), P())
    return jax.shard_map(
        on_device, mesh=mesh, in_specs=in_specs, out_specs=out_specs, check_vma=False
    )
```

```python
import functools
import math

import jax
import jax.numpy as jnp
from jax import lax
from jax.experimental import pallas as pl
from jax.experimental.pallas import tpu as pltpu
from jax.sharding import PartitionSpec as P

RB = 512
NT = 128
VMEM = 14 * 1024 * 1024
PARTS = (7, 4, 4, 1)
GROUPS = ((0,), (1,), (2, 3))
LOW, LOW_X, OWN, MATE, HIGH, HIGH_X = range(6)
IN_SMEM = pl.BlockSpec(memory_space=pltpu.SMEM)
IN_VMEM = pl.BlockSpec(memory_space=pltpu.VMEM)
IN_HBM = pl.BlockSpec(memory_space=pltpu.HBM)
PARAMS = pltpu.CompilerParams(vmem_limit_bytes=VMEM)
LIGHT = pl.CostEstimate(flops=0, bytes_accessed=0, transcendentals=0)


def columns(ref, start, size):
    return ref.at[:, :, pl.ds(pl.multiple_of(start, 128), size)]


def run(copies):
    for copy in copies:
        copy.start()
    for copy in copies:
        copy.wait()


def split_kernel(half, off, size, other, info, whole, out, sem):
    side = 1 - info[0] if other else info[0]
    run([pltpu.make_async_copy(columns(whole, side * half + off, size), out, sem)])


def split(info, whole, half, off, size, other):
    return pl.pallas_call(
        functools.partial(split_kernel, half, off, size, other),
        out_shape=jax.ShapeDtypeStruct((*whole.shape[:2], size), whole.dtype),
        in_specs=[IN_SMEM, IN_HBM],
        out_specs=IN_VMEM,
        scratch_shapes=[pltpu.SemaphoreType.DMA],
        compiler_params=PARAMS,
        cost_estimate=LIGHT,
        name="split_columns",
    )(info, whole)


def join_kernel(half, cuts, info, whole, theirs, *refs):
    outs, sems = refs[:-1], refs[-1]
    base = cuts[0][0]
    copies = []
    for n, (off, size) in enumerate(cuts):
        mine = columns(whole, info[0] * half + off, size)
        copies.append(pltpu.make_async_copy(mine, outs[n].at[0], sems.at[2 * n]))
        got = theirs.at[:, :, pl.ds(off - base, size)]
        copies.append(pltpu.make_async_copy(got, outs[n].at[1], sems.at[2 * n + 1]))
    run(copies)


def join(info, whole, theirs, half, cuts):
    return pl.pallas_call(
        functools.partial(join_kernel, half, cuts),
        out_shape=[
            jax.ShapeDtypeStruct((2, *theirs.shape[:2], size), theirs.dtype) for _, size in cuts
        ],
        in_specs=[IN_SMEM, IN_HBM, IN_VMEM],
        out_specs=[IN_VMEM] * len(cuts),
        scratch_shapes=[pltpu.SemaphoreType.DMA((2 * len(cuts),))],
        compiler_params=PARAMS,
        cost_estimate=LIGHT,
        name="join_blocks",
    )(info, whole, theirs)


def place_kernel(half, cuts, info, *refs):
    parts, whole, sems = refs[: 2 * len(cuts)], refs[-2], refs[-1]
    side = info[0]
    copies = []
    for n, (off, size) in enumerate(cuts):
        for m, at in ((2 * n, side), (2 * n + 1, 1 - side)):
            to = columns(whole, at * half + off, size)
            copies.append(pltpu.make_async_copy(parts[m], to, sems.at[m]))
    run(copies)


def place(info, pieces, whole, half):
    rows = pieces[0][0].shape[1]
    first = whole is None
    cuts = [(off, here.shape[2]) for here, _, off in pieces]
    parts = [part for here, there, _ in pieces for part in (here, there)]
    return pl.pallas_call(
        functools.partial(place_kernel, half, cuts),
        out_shape=jax.ShapeDtypeStruct((2, rows, 2 * half), parts[0].dtype),
        in_specs=[IN_SMEM] + [IN_VMEM] * len(parts) + ([] if first else [IN_HBM]),
        out_specs=IN_HBM,
        scratch_shapes=[pltpu.SemaphoreType.DMA((len(parts),))],
        input_output_aliases={} if first else {1 + len(parts): 0},
        compiler_params=PARAMS,
        cost_estimate=LIGHT,
        name="place_columns",
    )(info, *parts, *([] if first else [whole]))


def prepare_kernel(info, own, mate, resp, mask):
    rows = mask.shape[0] // 2
    none = None
    tables = (
        ((0, 1, 2, 3, 4, none), (none, 0, 1, 2, 3, 4)),
        ((0, none, 2, 1, 4, 3), (1, 0, 3, 2, none, 4)),
    )
    for which, params in ((0, own), (1, mate)):
        mask[which * rows : (which + 1) * rows, :] = params[2 * rows :, :rows].astype(jnp.float32).T
        line = slice(2 * which * rows, (2 * which + 1) * rows)
        line_im = slice((2 * which + 1) * rows, (2 * which + 2) * rows)
        for side in range(2):

            @pl.when(info[0] == side)
            def _(params=params, line=line, line_im=line_im, table=tables[side][which]):
                for slot, k in enumerate(table):
                    at = slice(slot * rows, (slot + 1) * rows)
                    at_im = slice((6 + slot) * rows, (7 + slot) * rows)
                    if k is None:
                        re = im = jnp.zeros((rows, rows), resp.dtype)
                    else:
                        re = params[:rows, k * rows : (k + 1) * rows]
                        im = params[rows : 2 * rows, k * rows : (k + 1) * rows]
                    resp[line, at] = re
                    resp[line, at_im] = -im
                    resp[line_im, at] = im
                    resp[line_im, at_im] = re


def prepare(info, own, mate, rows):
    blocks = own.shape[0] - 2 * rows
    return pl.pallas_call(
        prepare_kernel,
        out_shape=[
            jax.ShapeDtypeStruct((4 * rows, 12 * rows), own.dtype),
            jax.ShapeDtypeStruct((2 * rows, blocks), jnp.float32),
        ],
        in_specs=[IN_SMEM, IN_VMEM, IN_VMEM],
        out_specs=[IN_VMEM, IN_VMEM],
        compiler_params=PARAMS,
        cost_estimate=LIGHT,
        name="prepare_response",
    )(info, own, mate)


def chunk_kernel(conf, *refs):
    rows, size, stride, half, off, scale, layout, first, last = conf
    refs = list(refs)
    info, wave, resp, mask = (refs.pop(0) for _ in range(4))
    given = [refs.pop(0) for _ in range(max(ref for ref, _ in layout) + 1)]
    if not first:
        grad_in, corr_in = refs.pop(0), refs.pop(0)
    out_own, out_mate = refs.pop(0), refs.pop(0)
    if last:
        grad_own, grad_mate, corr_out = (refs.pop(0) for _ in range(3))
    else:
        grad_out, corr_out = refs.pop(0), refs.pop(0)
    ys, ms, sums, corrs = refs
    side, pos = info[0], info[1]
    even = side == 0
    col0 = side * half + off
    spans, at = [], 0
    while at < size:
        wide = RB if (off + at) % RB == 0 and at + RB <= size else RB // 2
        spans.append((at, at + wide))
        at += wide

    def record(slot, c, cols=slice(None)):
        ref, part = layout[slot]
        return given[ref][c, :, cols] if part is None else given[ref][part, c, :, cols]

    piece = min(RB // 2, rows * stride)

    def hit_slot(start):
        ahead = start // (rows * stride) - (pos - side - 2)
        inside = (ahead >= 0) & (ahead < 6)
        return inside, jnp.where(even, ahead, ahead + 1 - 2 * lax.rem(ahead, 2))

    def hits(start):
        shots = lax.broadcasted_iota(jnp.int32, (rows, piece), 0)
        cols = lax.rem(start, rows * stride) + lax.broadcasted_iota(jnp.int32, (rows, piece), 1)
        return shots * stride == cols

    for slot in range(6):
        at = slice(slot * rows, (slot + 1) * rows)
        for c in range(2):
            ys[at, c * size : (c + 1) * size] = record(slot, c)

    @pl.loop(0, size // piece)
    def _(t):
        inside, slot = hit_slot(col0 + t * piece)

        @pl.when(inside)
        def _():
            hit = hits(col0 + t * piece)
            at = pl.ds(pl.multiple_of(slot * rows, rows), rows)
            for c in range(2):
                cols = pl.ds(pl.multiple_of(c * size + t * piece, piece), piece)
                direct = jnp.where(hit, wave[c], 0.0)
                ys[at, cols] = (ys[at, cols].astype(jnp.float32) - direct).astype(jnp.bfloat16)

    across = (((1,), (1,)), ((), ()))
    corrs[...] = jnp.zeros_like(corrs) if first else corr_in[...]
    listed = mask[...]
    receiver_block = lax.broadcasted_iota(jnp.int32, listed.shape, 1)
    for low, high in spans:
        cols = slice(low, high)
        cols_im = slice(size + low, size + high)
        y = jnp.concatenate([ys[:, cols], ys[:, cols_im]], axis=0)
        fit = jnp.dot(resp[...], y, preferred_element_type=jnp.float32)
        here = receiver_block == (col0 + low) // RB
        covered = jnp.max(jnp.where(here, listed, 0.0), axis=1, keepdims=True)
        for which, slot, out in ((0, OWN, out_own), (1, MATE, out_mate)):
            weight = covered[which * rows : (which + 1) * rows]
            pair = []
            for c in range(2):
                at = 2 * which + c
                value = record(slot, c, cols).astype(jnp.float32) + fit[at * rows : (at + 1) * rows]
                pair.append((weight * value).astype(jnp.bfloat16))
                out[c, :, cols] = pair[c]
            at = slice(2 * which * rows, (2 * which + 1) * rows)
            ms[at, cols] = pair[0]
            ms[at, cols_im] = pair[1]
            at = slice((2 * which + 1) * rows, (2 * which + 2) * rows)
            ms[at, cols] = pair[1]
            ms[at, cols_im] = -pair[0]

    @pl.loop(0, size // piece)
    def _(t):
        inside, slot = hit_slot(col0 + t * piece)

        @pl.when(inside)
        def _():
            one = jnp.where(hits(col0 + t * piece), 1.0, 0.0).astype(jnp.bfloat16)
            cols = pl.ds(pl.multiple_of(t * piece, piece), piece)
            at_shots = lax.dot_general(ms[:, cols], one, across, preferred_element_type=jnp.float32)
            for c in range(2):
                at = pl.ds(pl.multiple_of((c * 6 + slot) * rows, rows), rows)
                terms = (resp[:, at].astype(jnp.float32) * at_shots).reshape(-1, 8, rows)
                corrs[c] -= jnp.sum(terms, axis=0)

    total = lax.dot_general(ys[...], ms[...], across, preferred_element_type=jnp.float32)
    if not first:
        total = grad_in[...] + total
    if not last:
        grad_out[...] = total
        corr_out[...] = corrs[...]
        return
    sums[...] = total
    orders = (
        (grad_own, (LOW, (LOW_X, MATE), OWN, (MATE, HIGH_X), HIGH)),
        (grad_mate, (LOW_X, (OWN, LOW), MATE, (HIGH, OWN), HIGH_X)),
    )
    for which, (out, order) in enumerate(orders):
        for c in range(2):
            at = slice((2 * which + c) * rows, (2 * which + c + 1) * rows)
            for k, slot in enumerate(order):
                pair = slot if isinstance(slot, tuple) else (slot,)
                value = [sums[s * rows : (s + 1) * rows, at] for s in pair]
                value = value[0] if len(pair) == 1 else jnp.where(even, *value)
                out[c, :, k * rows : (k + 1) * rows] = value.T
    corr = [jnp.sum(jnp.sum(corrs[c], axis=0, keepdims=True), axis=1, keepdims=True) for c in range(2)]
    turns = lax.rem((info[2] + 1) * lax.broadcasted_iota(jnp.int32, (1, NT), 1), NT)
    phase = turns.astype(jnp.float32) * (2.0 * math.pi / NT)
    corr_out[...] = (corr[0] * jnp.cos(phase) - corr[1] * jnp.sin(phase)) * scale


def chunk(consts, arrays, layout, carry, off, size, half, stride, rows, band, last):
    info, wave, resp, mask = consts
    first = carry is None
    scale = 1.0 / math.sqrt(2 * half // stride * band)
    conf = (rows, size, stride, half, off, scale, layout, first, last)
    args = [info, wave, resp, mask, *arrays]
    in_specs = [IN_SMEM, IN_SMEM] + [IN_VMEM] * (len(args) - 2)
    aliases = {}
    if not first:
        if not last:
            aliases = {len(args): 2, len(args) + 1: 3}
        args += list(carry)
        in_specs += [IN_VMEM, IN_VMEM]
    if last:
        sums = [jax.ShapeDtypeStruct((2, rows, band), jnp.float32)] * 2
        sums.append(jax.ShapeDtypeStruct((1, NT), jnp.float32))
    else:
        sums = [jax.ShapeDtypeStruct((6 * rows, 4 * rows), jnp.float32)]
        sums.append(jax.ShapeDtypeStruct((2, 8, rows), jnp.float32))
    out_shape = [jax.ShapeDtypeStruct((2, rows, size), jnp.bfloat16)] * 2 + sums
    return pl.pallas_call(
        functools.partial(chunk_kernel, conf),
        out_shape=out_shape,
        in_specs=in_specs,
        out_specs=[IN_VMEM] * len(out_shape),
        scratch_shapes=[
            pltpu.VMEM((6 * rows, 2 * size), jnp.bfloat16),
            pltpu.VMEM((4 * rows, 2 * size), jnp.bfloat16),
            pltpu.VMEM((6 * rows, 4 * rows), jnp.float32),
            pltpu.VMEM((2, 8, rows), jnp.float32),
        ],
        input_output_aliases=aliases,
        compiler_params=PARAMS,
        cost_estimate=LIGHT,
        name="residual_chunk",
    )(*args)


def total_over(value, axis, steps):
    size = lax.axis_size(axis)
    for step in steps:
        value = value + lax.ppermute(value, axis, [(i, i ^ step) for i in range(size)])
    return value


def after(value, *others):
    others = [a for a in others if a is not None]
    return lax.optimization_barrier((value, *others))[0] if others else value


def on_device(data, primaries, wavelet, cover_ids, cover_counts):
    record = data[0]
    _, rows, width = record.shape
    band = primaries.shape[3]
    shots, freqs = lax.axis_size("shot"), lax.axis_size("freq")
    shot_count = shots * rows
    stride = width // shot_count
    half = width // 2
    position = lax.axis_index("shot").astype(jnp.int32)
    freq_index = lax.axis_index("freq").astype(jnp.int32)
    info = jnp.stack([position % 2, position, freq_index])
    cuts, off = [], 0
    for part in PARTS:
        size = part * (half // sum(PARTS))
        cuts.append((off, size))
        off += size
    steps = len(cuts)

    def swap(a):
        return lax.ppermute(a, "shot", [(s, s ^ 1) for s in range(shots)])

    def neighbours(a):
        return [
            lax.ppermute(a, "shot", [(s, s + d) for s in range(shots) if 0 <= s + d < shots])
            for d in (2, -2)
        ]

    swapped = []
    for n, group in enumerate(GROUPS):
        off, size = cuts[group[0]][0], sum(cuts[m][1] for m in group)
        piece = split(info, record, half, off, size, True)
        swapped.append(swap(after(piece, *swapped[n - 2 : n - 1]) if n >= 2 else piece))
    mine = split(info, record, half, *cuts[0], False)
    near = neighbours(mine)

    listed = jnp.arange(cover_ids.shape[1], dtype=jnp.int32)[None, :] < cover_counts[:, None]
    ids = jnp.arange(width // RB, dtype=jnp.int32)
    covered = jnp.any((cover_ids[:, :, None] == ids) & listed[:, :, None], axis=1)
    covered = jnp.pad(covered.T.astype(jnp.bfloat16), ((0, 0), (0, band - rows)))
    params = jnp.concatenate([primaries[0].reshape(2 * rows, band), covered], axis=0)
    params_there = swap(after(params, swapped[0]))
    resp, mask = prepare(info, params, params_there, rows)
    consts = (info, wavelet[0], resp, mask)

    far = neighbours(swapped[0])
    arrays = [near[0], far[0], mine, swapped[0], near[1], far[1]]
    layout = tuple((n, None) for n in range(6))
    both = [None]
    carry = whole = None
    sent = []
    for n, (off, size) in enumerate(cuts):
        if n + 1 < steps:
            if n + 1 == len(both):
                group = GROUPS[n + 1]
                both += join(info, record, swapped[n + 1], half, [cuts[m] for m in group])
            ahead = neighbours(both[n + 1])
        gate = list(both[n + 1 : n + 2])
        if n >= 2:
            whole = place(info, sent[n - 2 : n - 1], whole, half)
            info_now, whole = lax.optimization_barrier((info, whole, *gate))[:2]
        else:
            info_now = after(info, *gate)
        here, there, *grad, corr = chunk(
            (info_now, *consts[1:]),
            arrays, layout, carry, off, size, half, stride, rows, band, n == steps - 1,
        )
        carry = (grad[0], corr)
        sent.append((here, swap(there), off))
        if n + 1 < steps:
            arrays = [both[n + 1], *ahead]
            layout = ((1, 0), (1, 1), (0, 0), (0, 1), (2, 0), (2, 1))
    whole = place(info, sent[-2:], whole, half)
    gradient = grad[0] + swap(grad[1])
    if shots & (shots - 1) or freqs & (freqs - 1):
        total = lax.psum(corr, ("shot", "freq"))
    else:
        total = total_over(corr, "shot", [2**i for i in range(1, shots.bit_length() - 1)])
        total = total_over(total, "freq", [2**i for i in range(freqs.bit_length() - 1)])
        total = total_over(total, "shot", [1])
    return (whole[None], gradient[None], total[0])


def solution(mesh):
    in_specs = (
        P("freq", None, "shot", None),
        P("freq", None, "shot", None),
        P("freq", None),
        P("shot", None),
        P("shot"),
    )
    out_specs = (P("freq", None, "shot", None), P("freq", None, "shot", None), P())
    return jax.shard_map(
        on_device, mesh=mesh, in_specs=in_specs, out_specs=out_specs, check_vma=False
    )
```
